128 devices in a mesh: grp: 4 (over x), seq: 32 (over y, z, core).
Axes of the slice: x: 4, y: 4, z: 4, core: 2. Of those that a mesh axis runs over, the one named last changes fastest.
Arguments:
- queries: bfloat16 [65536, 2048], P(('grp', 'seq')), may hold values from -6 to 6
- key_vectors: bfloat16 [65536, 2048], P(('grp', 'seq')), may hold values from -6 to 6
- value_vectors: bfloat16 [65536, 2048], P(('grp', 'seq')), may hold values from -6 to 6
- forward_output: bfloat16 [65536, 2048], P(('grp', 'seq')), may hold values from -6 to 6
- output_grad: bfloat16 [65536, 2048], P(('grp', 'seq')), may hold values from -6 to 6
- log_normalizer: float32 [16, 65536], P(None, ('grp', 'seq')), may hold values from -1 to 12
- piece_start: int32 [65536], P(('grp', 'seq')), may hold values from 0 to 65535, as said below
- bar_window: int32 [65536], P(('grp', 'seq')), may hold values from 32 to 512, as said below
Outputs:
- query_grad: bfloat16 [65536, 2048], P(('grp', 'seq'))
- key_grad: bfloat16 [65536, 2048], P(('grp', 'seq'))
- value_grad: bfloat16 [65536, 2048], P(('grp', 'seq'))
The draws below stay inside these ranges and needn't reach their ends.
Inputs may be any that keep to these rules, and one draw needn't show every extreme that they name: piece_start[t] is the first position of the piece that holds token t: it never falls along the sequence, is at most t, and equals t exactly where a piece begins; positions 0 and 65535 begin pieces. `bar_window`: a multiple of 32, the same for all tokens of one piece; the piece at position 0 has 512.
All inputs are finite; a program needn't handle non-finite values.
Results may differ from the reference program's by a relative error of at most 0.0045.
The reference program's roundings to bfloat16 on the way count: a program that leaves them out, or rounds other values in their place, can miss the bound.
Values may be sent and summed in bfloat16 or wider, within the bound.
A program may use at most 256 MiB of HBM per device.

```python
import jax
import jax.numpy as jnp
from jax import lax

HEADS = 16
BAR = 32
ROWS = 512
D = 2048
TOKENS = 65536


def piece_layout(key):
    region_key, flag_key, window_key = jax.random.split(key, 3)
    exponents = jax.random.randint(region_key, (TOKENS // 128,), 3, 14)
    per_token = jnp.repeat(exponents, 128)
    random_bits = jax.random.randint(flag_key, (TOKENS,), 0, 8192)
    threshold = jnp.left_shift(jnp.ones((TOKENS,), jnp.int32), 13 - per_token)
    positions = jnp.arange(TOKENS, dtype=jnp.int32)
    begins = (random_bits < threshold) | (positions == 0) | (positions == TOKENS - 1)
    starts = lax.cummax(jnp.where(begins, positions, 0), axis=0)
    window_units = jax.random.randint(window_key, (TOKENS,), 1, ROWS // BAR + 1)
    window_units = window_units.at[0].set(ROWS // BAR)
    windows = BAR * window_units[starts]
    return (starts, windows)


def draw_piece_start(key, part):
    starts, windows = piece_layout(key)
    return starts


def draw_bar_window(key, part):
    starts, windows = piece_layout(key)
    return windows


def draw_log_normalizer(key, part):
    starts, windows = piece_layout(key)
    key = jax.random.fold_in(key, 3)
    positions = jnp.arange(TOKENS, dtype=jnp.int32)
    counts = jnp.minimum(positions - starts + 1, windows).astype(jnp.float32)
    jitter = jnp.clip(0.3 * jax.random.normal(key, (HEADS, TOKENS), jnp.float32), -0.9, 0.9)
    return jnp.log(counts)[None, :] + 0.5 + jitter


def levels(own_key, dims, shards, smallest, largest):
    def one(axis_at, shards_of):
        draws = jax.random.uniform(jax.random.fold_in(jax.random.fold_in(own_key, 6), axis_at), (shards_of,), jnp.float32, smallest / len(shards), largest / len(shards))
        return jnp.repeat(jnp.exp(draws), dims[axis_at] // shards_of).reshape((-1,) + (1,) * (len(dims) - axis_at - 1))

    factor_of = one(*shards[0])
    for cut in shards[1:]:
        factor_of = factor_of * one(*cut)
    return factor_of


def bell_draw(rng, shape, scale, reach, shards=(), kind=jnp.bfloat16):
    loudness = levels(rng, shape, shards, -0.22, 0.18) if shards else 1.0
    values = jax.random.normal(rng, shape, jnp.float32) * scale * loudness
    return jnp.minimum(jnp.maximum(values, -reach), reach).astype(kind)


def setup_inputs(seed: int = 0) -> dict:
    keys = jax.random.split(jax.random.key(seed), 9)
    return {
        "queries": bell_draw(keys[0], (TOKENS, D), 1.0, 6.0, ((0, 128),)),
        "key_vectors": bell_draw(keys[1], (TOKENS, D), 1.0, 6.0, ((0, 128),)),
        "value_vectors": bell_draw(keys[2], (TOKENS, D), 1.0, 6.0, ((0, 128),)),
        "forward_output": bell_draw(keys[3], (TOKENS, D), 1.0, 6.0, ((0, 128),)),
        "output_grad": bell_draw(keys[4], (TOKENS, D), 1.0, 6.0, ((0, 128),)),
        "log_normalizer": draw_log_normalizer(jax.random.fold_in(keys[8], 71), 0),
        "piece_start": draw_piece_start(jax.random.fold_in(keys[8], 71), 0),
        "bar_window": draw_bar_window(jax.random.fold_in(keys[8], 71), 0),
    }


def visible_pairs(query_start, query_window, key_start, offset):
    grid_shape = (query_start.shape[0], key_start.shape[0])
    distance = offset + lax.broadcasted_iota(jnp.int32, grid_shape, 0) - lax.broadcasted_iota(jnp.int32, grid_shape, 1)
    same_piece = query_start[:, None] == key_start[None, :]
    return same_piece & (distance >= 0) & (distance < query_window[:, None])


def block_grads(queries, output_grad, normalizer, delta_rows, key_vectors, value_vectors, visible):
    head_count = normalizer.shape[0]
    model_width = queries.shape[1]
    head_size = model_width // head_count
    softmax_scale = head_size ** -0.5
    rows_here = queries.shape[0]
    columns = key_vectors.shape[0]
    query_heads = queries.astype(jnp.float32).reshape(rows_here, head_count, head_size)
    grad_heads = output_grad.astype(jnp.float32).reshape(rows_here, head_count, head_size)
    key_heads = key_vectors.astype(jnp.float32).reshape(columns, head_count, head_size)
    value_heads = value_vectors.astype(jnp.float32).reshape(columns, head_count, head_size)
    highest = lax.Precision.HIGHEST
    scores = jnp.einsum("qhd,khd->hqk", query_heads, key_heads, precision=highest) * softmax_scale
    softmax_probs = jnp.where(visible[None], jnp.exp(scores - normalizer[:, :, None]), 0.0)
    prob_grad = jnp.einsum("qhd,khd->hqk", grad_heads, value_heads, precision=highest)
    score_grad = softmax_probs * (prob_grad - delta_rows[:, :, None])
    rounded_probs = softmax_probs.astype(jnp.bfloat16).astype(jnp.float32)
    rounded_grad = score_grad.astype(jnp.bfloat16).astype(jnp.float32)
    value_part = jnp.einsum("hqk,qhd->khd", rounded_probs, grad_heads, precision=highest)
    key_part = jnp.einsum("hqk,qhd->khd", rounded_grad, query_heads, precision=highest) * softmax_scale
    query_part = jnp.einsum("hqk,khd->qhd", rounded_grad, key_heads, precision=highest) * softmax_scale
    return (query_part.reshape(rows_here, model_width), key_part.reshape(columns, model_width), value_part.reshape(columns, model_width))


def guarded(queries, output_grad, normalizer, delta_rows, key_vectors, value_vectors, visible):
    def compute(operands):
        return block_grads(*operands)

    def nothing(operands):
        model_width = queries.shape[1]
        return (jnp.zeros((queries.shape[0], model_width), jnp.float32), jnp.zeros((key_vectors.shape[0], model_width), jnp.float32), jnp.zeros((key_vectors.shape[0], model_width), jnp.float32))

    operands = (queries, output_grad, normalizer, delta_rows, key_vectors, value_vectors, visible)
    return lax.cond(jnp.any(visible), compute, nothing, operands)


def reference(queries, key_vectors, value_vectors, forward_output, output_grad, log_normalizer, piece_start, bar_window):
    tokens, model_width = queries.shape
    head_count = log_normalizer.shape[0]
    head_size = model_width // head_count
    block_count = tokens // ROWS
    products = forward_output.astype(jnp.float32) * output_grad.astype(jnp.float32)
    delta_all = jnp.sum(products.reshape(tokens, head_count, head_size), axis=2).T

    def rows_of(array, block_index):
        return lax.dynamic_slice_in_dim(array, block_index * ROWS, ROWS, 0)

    def columns_of(array, block_index):
        return lax.dynamic_slice_in_dim(array, block_index * ROWS, ROWS, 1)

    def one_block(block_index):
        later_block = jnp.minimum(block_index + 1, block_count - 1).astype(jnp.int32)
        has_later = block_index + 1 < block_count
        local_visible = visible_pairs(rows_of(piece_start, block_index), rows_of(bar_window, block_index), rows_of(piece_start, block_index), 0)
        local_part = guarded(rows_of(queries, block_index), rows_of(output_grad, block_index), columns_of(log_normalizer, block_index), columns_of(delta_all, block_index), rows_of(key_vectors, block_index), rows_of(value_vectors, block_index), local_visible)
        shared_visible = visible_pairs(rows_of(piece_start, later_block), rows_of(bar_window, later_block), rows_of(piece_start, block_index), ROWS) & has_later
        shared_part = guarded(rows_of(queries, later_block), rows_of(output_grad, later_block), columns_of(log_normalizer, later_block), columns_of(delta_all, later_block), rows_of(key_vectors, block_index), rows_of(value_vectors, block_index), shared_visible)
        key_total = (local_part[1] + shared_part[1]).astype(jnp.bfloat16)
        value_total = (local_part[2] + shared_part[2]).astype(jnp.bfloat16)
        return local_part[0], shared_part[0], key_total, value_total

    local_query, shared_query, key_grad, value_grad = lax.map(one_block, jnp.arange(block_count, dtype=jnp.int32))
    moved = jnp.concatenate([jnp.zeros_like(shared_query[:1]), shared_query[:-1]], axis=0)
    query_grad = (local_query + moved).astype(jnp.bfloat16).reshape(tokens, model_width)
    return (query_grad, key_grad.reshape(tokens, model_width), value_grad.reshape(tokens, model_width))
```

```python
import functools

import jax
import jax.numpy as jnp
from jax import lax
from jax.experimental import pallas as pl
from jax.experimental.pallas import tpu as pltpu
from jax.sharding import PartitionSpec as P

MESH = pl.DeviceIdType.MESH
LOG2E = 1.4426950408889634
HEAD = 128
LAG = 3
AHEAD = 2


def dot(a, b, contract):
    return lax.dot_general(
        a, b, ((contract[:1], contract[1:]), ((), ())), preferred_element_type=jnp.float32
    )


def kernel(
    groups,
    group_size,
    heads,
    q_hbm,
    k_hbm,
    v_hbm,
    o_hbm,
    g_hbm,
    lse_hbm,
    start_hbm,
    window_hbm,
    dq_out,
    dk_out,
    dv_out,
    q_own,
    k_own,
    v_own,
    o_own,
    g_own,
    lse_own,
    start_own,
    window_own,
    stats_own,
    stats_next,
    q_next,
    g_next,
    dq_own,
    dq_sent,
    dq_got,
    load_sem,
    send_sem,
    recv_sem,
    stats_sem,
    back_send_sem,
    back_recv_sem,
):
    rows = q_hbm.shape[0]
    half = rows // 2
    count = groups * group_size
    here = lax.axis_index("grp") * group_size + lax.axis_index("seq")

    def place(index):
        return (index // group_size, lax.rem(index, group_size))

    before = place(lax.rem(here + count - 1, count))
    after = place(lax.rem(here + 1, count))

    def load(number, source, target):
        return pltpu.make_async_copy(source, target, load_sem.at[number])

    loads = [
        load(0, o_hbm, o_own),
        load(1, g_hbm, g_own),
        load(2, lse_hbm, lse_own),
        load(3, start_hbm, start_own),
        load(4, window_hbm, window_own),
        load(5, q_hbm, q_own),
        load(6, k_hbm, k_own),
        load(7, v_hbm, v_own),
    ]
    for copy in loads:
        copy.start()

    barrier = pltpu.get_barrier_semaphore()
    for neighbour in (before, after):
        pl.semaphore_signal(barrier, inc=1, device_id=neighbour, device_id_type=MESH)
    pl.semaphore_wait(barrier, 2)

    def columns(h):
        return pl.ds(pl.multiple_of(h * HEAD, HEAD), HEAD)

    def to_before(h):
        return [
            pltpu.make_async_remote_copy(
                src_ref=source.at[:, columns(h)],
                dst_ref=target.at[h],
                send_sem=send_sem.at[number, h],
                recv_sem=recv_sem.at[number, h],
                device_id=before,
                device_id_type=MESH,
            )
            for number, (source, target) in enumerate(((q_hbm, q_next), (g_hbm, g_next)))
        ]

    def to_after(h):
        return pltpu.make_async_remote_copy(
            src_ref=dq_sent.at[h],
            dst_ref=dq_got.at[h],
            send_sem=back_send_sem.at[h],
            recv_sem=back_recv_sem.at[h],
            device_id=after,
            device_id_type=MESH,
        )

    for h in range(AHEAD):
        for copy in to_before(h):
            copy.start()

    for copy in loads[:5]:
        copy.wait()
    positions = lax.broadcasted_iota(jnp.int32, (1, rows), 1)
    lowest = (
        jnp.maximum(
            start_own[...].reshape(1, rows) - here * rows,
            positions - window_own[...].reshape(1, rows) + 1,
        )
    ).astype(jnp.float32)
    stats_own[0:heads, :] = lse_own[...] * LOG2E
    model = heads * HEAD
    picks = (
        lax.broadcasted_iota(jnp.int32, (heads, model), 1) // HEAD
        == lax.broadcasted_iota(jnp.int32, (heads, model), 0)
    ).astype(jnp.float32).astype(jnp.bfloat16)
    for r in range(0, rows, 128):
        products = o_own[r : r + 128, :].astype(jnp.float32) * g_own[r : r + 128, :].astype(
            jnp.float32
        )
        high = products.astype(jnp.bfloat16)
        low = (products - high.astype(jnp.float32)).astype(jnp.bfloat16)
        stats_own[heads : 2 * heads, r : r + 128] = dot(picks, high, (1, 1)) + dot(
            picks, low, (1, 1)
        )
    stats_own[2 * heads : 2 * heads + 8, :] = jnp.broadcast_to(lowest + rows, (8, rows))
    stats_copy = pltpu.make_async_remote_copy(
        src_ref=stats_own,
        dst_ref=stats_next,
        send_sem=stats_sem.at[0],
        recv_sem=stats_sem.at[1],
        device_id=before,
        device_id_type=MESH,
    )
    stats_copy.start()
    for copy in loads[5:]:
        copy.wait()

    scale = HEAD**-0.5

    def pair_block(k, v, q, g, lse, delta, mask):
        s = dot(k, q, (1, 1)) * (scale * LOG2E) - lse
        p = jnp.where(mask, jnp.exp2(s), 0.0)
        ds = p * (dot(v, g, (1, 1)) - delta)
        return p.astype(jnp.bfloat16), ds.astype(jnp.bfloat16)

    def finish(h):
        to_after(h).wait_recv()
        total = dq_own[h] + dq_got[h].astype(jnp.float32)
        dq_out[:, columns(h)] = total.T.astype(jnp.bfloat16)

    key_at = lax.broadcasted_iota(jnp.int32, (half, half), 0).astype(jnp.float32)
    query_at = lax.broadcasted_iota(jnp.int32, (half, half), 1).astype(jnp.float32)
    lo, hi = slice(0, half), slice(half, rows)

    def one_head(h, carry):
        @pl.when(h + AHEAD < heads)
        def _():
            for copy in to_before(h):
                copy.wait_send()
            for copy in to_before(h + AHEAD):
                copy.start()

        cols = columns(h)
        k, v, q, g = k_own[:, cols], v_own[:, cols], q_own[:, cols], g_own[:, cols]
        kt = k.T
        lse = stats_own[pl.ds(h, 1), :]
        delta = stats_own[pl.ds(heads + h, 1), :]
        bound = stats_own[2 * heads : 2 * heads + 1, :] - rows

        def local(us, ts, diagonal):
            mask = key_at + us.start >= bound[:, ts]
            if diagonal:
                mask = mask & (key_at <= query_at)
            return pair_block(k[us], v[us], q[ts], g[ts], lse[:, ts], delta[:, ts], mask)

        p00, s00 = local(lo, lo, True)
        p01, s01 = local(lo, hi, False)
        p11, s11 = local(hi, hi, True)
        dv0 = dot(p00, g[lo], (1, 0)) + dot(p01, g[hi], (1, 0))
        dv1 = dot(p11, g[hi], (1, 0))
        dk0 = dot(s00, q[lo], (1, 0)) + dot(s01, q[hi], (1, 0))
        dk1 = dot(s11, q[hi], (1, 0))
        dq_own[h, :, lo] = dot(kt[:, lo], s00, (1, 0)) * scale
        dq_own[h, :, hi] = (dot(kt[:, lo], s01, (1, 0)) + dot(kt[:, hi], s11, (1, 0))) * scale

        @pl.when(h == 0)
        def _():
            stats_copy.wait_recv()

        for copy in to_before(h):
            copy.wait_recv()
        qn, gn = q_next[h], g_next[h]
        lse_n = stats_next[pl.ds(h, 1), :]
        delta_n = stats_next[pl.ds(heads + h, 1), :]
        bound_n = stats_next[2 * heads : 2 * heads + 1, :]

        def shared(us, ts):
            mask = key_at + us.start >= bound_n[:, ts]
            return pair_block(k[us], v[us], qn[ts], gn[ts], lse_n[:, ts], delta_n[:, ts], mask)

        p00, s00 = shared(lo, lo)
        p10, s10 = shared(hi, lo)
        p11, s11 = shared(hi, hi)
        dq_sent[h, :, lo] = (
            (dot(kt[:, lo], s00, (1, 0)) + dot(kt[:, hi], s10, (1, 0))) * scale
        ).astype(jnp.bfloat16)
        dq_sent[h, :, hi] = (dot(kt[:, hi], s11, (1, 0)) * scale).astype(jnp.bfloat16)
        to_after(h).start()
        dv0 += dot(p00, gn[lo], (1, 0))
        dv1 += dot(p10, gn[lo], (1, 0)) + dot(p11, gn[hi], (1, 0))
        dk0 += dot(s00, qn[lo], (1, 0))
        dk1 += dot(s10, qn[lo], (1, 0)) + dot(s11, qn[hi], (1, 0))
        dv_out[lo, cols] = dv0.astype(jnp.bfloat16)
        dv_out[hi, cols] = dv1.astype(jnp.bfloat16)
        dk_out[lo, cols] = (dk0 * scale).astype(jnp.bfloat16)
        dk_out[hi, cols] = (dk1 * scale).astype(jnp.bfloat16)

        @pl.when(h >= LAG)
        def _():
            finish(h - LAG)

        return carry

    lax.fori_loop(0, heads, one_head, 0)
    lax.fori_loop(heads - LAG, heads, lambda h, c: (finish(h), c)[1], 0)
    stats_copy.wait_send()

    def drain(h, carry):
        to_after(h).wait_send()

        @pl.when(h + AHEAD >= heads)
        def _():
            for copy in to_before(h):
                copy.wait_send()

        return carry

    lax.fori_loop(0, heads, drain, 0)


def solution(mesh):
    groups, group_size = mesh.shape["grp"], mesh.shape["seq"]

    def local(q, k, v, o, g, lse, start, window):
        rows, model = q.shape
        heads = lse.shape[0]
        block = jax.ShapeDtypeStruct((rows, model), jnp.bfloat16)
        whole = pltpu.VMEM((rows, model), jnp.bfloat16)
        per_head = pltpu.VMEM((heads, rows, HEAD), jnp.bfloat16)
        turned = pltpu.VMEM((heads, HEAD, rows), jnp.bfloat16)
        stats = pltpu.VMEM((2 * heads + 8, rows), jnp.float32)
        return pl.pallas_call(
            functools.partial(kernel, groups, group_size, heads),
            out_shape=(block, block, block),
            in_specs=[pl.BlockSpec(memory_space=pl.ANY)] * 8,
            out_specs=(pl.BlockSpec(memory_space=pltpu.VMEM),) * 3,
            scratch_shapes=[
                whole,
                whole,
                whole,
                whole,
                whole,
                pltpu.VMEM((heads, rows), jnp.float32),
                pltpu.VMEM((rows,), jnp.int32),
                pltpu.VMEM((rows,), jnp.int32),
                stats,
                stats,
                per_head,
                per_head,
                pltpu.VMEM((heads, HEAD, rows), jnp.float32),
                turned,
                turned,
                pltpu.SemaphoreType.DMA((8,)),
                pltpu.SemaphoreType.DMA((2, heads)),
                pltpu.SemaphoreType.DMA((2, heads)),
                pltpu.SemaphoreType.DMA((2,)),
                pltpu.SemaphoreType.DMA((heads,)),
                pltpu.SemaphoreType.DMA((heads,)),
            ],
            compiler_params=pltpu.CompilerParams(
                collective_id=0, has_side_effects=True, vmem_limit_bytes=56 * 2**20
            ),
        )(q, k, v, o, g, lse, start, window)

    block = P(("grp", "seq"), None)
    return jax.shard_map(
        local,
        mesh=mesh,
        in_specs=(block,) * 5 + (P(None, ("grp", "seq")),) + (P(("grp", "seq")),) * 2,
        out_specs=(block,) * 3,
        check_vma=False,
    )
```

```python
import functools

import jax
import jax.numpy as jnp
from jax import lax
from jax.experimental import pallas as pl
from jax.experimental.pallas import tpu as pltpu
from jax.sharding import PartitionSpec as P

MESH = pl.DeviceIdType.MESH
LOG2E = 1.4426950408889634
HEAD = 128
LEAD = 2
AHEAD = 3
LAG = 3
HIDDEN = -1e30


def dot(a, b, contract):
    return lax.dot_general(
        a, b, ((contract[:1], contract[1:]), ((), ())), preferred_element_type=jnp.float32
    )


def kernel(
    groups,
    group_size,
    heads,
    q_hbm,
    k_hbm,
    v_hbm,
    o_hbm,
    g_hbm,
    lse_hbm,
    start_hbm,
    window_hbm,
    dq_out,
    dk_out,
    dv_out,
    q_own,
    k_own,
    v_own,
    g_own,
    o_all,
    g_all,
    lse_own,
    start_own,
    window_own,
    stats_own,
    stats_next,
    bias,
    q_next,
    g_next,
    dk_part,
    dv_part,
    dq_own,
    dq_sent,
    dq_got,
    load_sem,
    head_sem,
    send_sem,
    recv_sem,
    stats_sem,
    back_send_sem,
    back_recv_sem,
):
    rows = q_hbm.shape[0]
    half = rows // 2
    count = groups * group_size
    here = lax.axis_index("grp") * group_size + lax.axis_index("seq")
    has_before, has_after = here > 0, here < count - 1
    scale = HEAD**-0.5
    lo, hi = slice(0, half), slice(half, rows)

    def place(index):
        return (index // group_size, lax.rem(index, group_size))

    before = place(lax.rem(here + count - 1, count))
    after = place(lax.rem(here + 1, count))

    def columns(h):
        return pl.ds(pl.multiple_of(h * HEAD, HEAD), HEAD)

    def head_load(h, number):
        source, target = ((q_hbm, q_own), (g_hbm, g_own), (k_hbm, k_own), (v_hbm, v_own))[number]
        return pltpu.make_async_copy(
            source.at[:, columns(h)], target.at[h], head_sem.at[number, h]
        )

    def to_before(h):
        return [
            pltpu.make_async_remote_copy(
                src_ref=source.at[h],
                dst_ref=target.at[h],
                send_sem=send_sem.at[number, h],
                recv_sem=recv_sem.at[number, h],
                device_id=before,
                device_id_type=MESH,
            )
            for number, (source, target) in enumerate(((q_own, q_next), (g_own, g_next)))
        ]

    def to_after(h):
        return pltpu.make_async_remote_copy(
            src_ref=dq_sent.at[h],
            dst_ref=dq_got.at[h],
            send_sem=back_send_sem.at[h],
            recv_sem=back_recv_sem.at[h],
            device_id=after,
            device_id_type=MESH,
        )

    stats_copy = pltpu.make_async_remote_copy(
        src_ref=stats_own,
        dst_ref=stats_next,
        send_sem=stats_sem.at[0],
        recv_sem=stats_sem.at[1],
        device_id=before,
        device_id_type=MESH,
    )

    whole_loads = [
        pltpu.make_async_copy(source, target, load_sem.at[number])
        for number, (source, target) in enumerate(
            (
                (o_hbm, o_all),
                (g_hbm, g_all),
                (lse_hbm, lse_own),
                (start_hbm, start_own),
                (window_hbm, window_own),
            )
        )
    ]
    head_load(0, 0).start()
    head_load(0, 1).start()
    for copy in whole_loads:
        copy.start()

    def start_loads(h, carry):
        for number in range(4):
            if number < 2:

                @pl.when(h > 0)
                def _():
                    head_load(h, number).start()

            else:
                head_load(h, number).start()
        return carry

    lax.fori_loop(0, heads, start_loads, 0)

    barrier = pltpu.get_barrier_semaphore()
    for neighbour in (before, after):
        pl.semaphore_signal(barrier, inc=1, device_id=neighbour, device_id_type=MESH)
    pl.semaphore_wait(barrier, 2)

    def admit(h):
        head_load(h, 0).wait()
        head_load(h, 1).wait()

        @pl.when(has_before)
        def _():
            for copy in to_before(h):
                copy.start()

    admit(0)

    for copy in whole_loads:
        copy.wait()
    positions = lax.broadcasted_iota(jnp.int32, (1, rows), 1)
    lowest = jnp.maximum(
        start_own[...].reshape(1, rows) - here * rows,
        positions - window_own[...].reshape(1, rows) + 1,
    )
    stats_own[0:heads, :] = lse_own[...] * LOG2E
    model = heads * HEAD
    picks = (
        lax.broadcasted_iota(jnp.int32, (heads, model), 1) // HEAD
        == lax.broadcasted_iota(jnp.int32, (heads, model), 0)
    ).astype(jnp.float32).astype(jnp.bfloat16)
    for r in range(0, rows, 128):
        products = o_all[r : r + 128, :].astype(jnp.float32) * g_all[r : r + 128, :].astype(
            jnp.float32
        )
        high = products.astype(jnp.bfloat16)
        low = (products - high.astype(jnp.float32)).astype(jnp.bfloat16)
        stats_own[heads : 2 * heads, r : r + 128] = dot(picks, high, (1, 1)) + dot(
            picks, low, (1, 1)
        )
    stats_own[2 * heads : 2 * heads + 8, :] = jnp.broadcast_to(
        (lowest + rows).astype(jnp.float32), (8, rows)
    )

    @pl.when(has_before)
    def _():
        stats_copy.start()

    for h in range(1, AHEAD):
        admit(h)

    key_at = lax.broadcasted_iota(jnp.int32, (half, half), 0)
    query_at = lax.broadcasted_iota(jnp.int32, (half, half), 1)

    def hidden_where_not(mask):
        return jnp.where(mask, 0.0, HIDDEN)

    bias[0] = hidden_where_not((key_at >= lowest[:, lo]) & (key_at <= query_at))
    bias[1] = hidden_where_not(key_at >= lowest[:, hi])
    bias[2] = hidden_where_not((key_at + half >= lowest[:, hi]) & (key_at <= query_at))

    def pair_block(k, v, q, g, lse, delta, number):
        s = dot(k, q, (1, 1)) * (scale * LOG2E) + bias[number]
        p = jnp.exp2(s - lse)
        ds = p * (dot(v, g, (1, 1)) - delta)
        return p.astype(jnp.bfloat16), ds.astype(jnp.bfloat16)

    def local(h):
        k, v, q, g = k_own[h], v_own[h], q_own[h], g_own[h]
        kt = k.T
        lse = stats_own[pl.ds(h, 1), :]
        delta = stats_own[pl.ds(heads + h, 1), :]

        def block(us, ts, number):
            return pair_block(k[us], v[us], q[ts], g[ts], lse[:, ts], delta[:, ts], number)

        p00, s00 = block(lo, lo, 0)
        p01, s01 = block(lo, hi, 1)
        p11, s11 = block(hi, hi, 2)
        slot = lax.rem(h, LEAD + 1)
        dv_part[slot, lo] = dot(jnp.concatenate([p00, p01], axis=1), g, (1, 0))
        dv_part[slot, hi] = dot(p11, g[hi], (1, 0))
        dk_part[slot, lo] = dot(jnp.concatenate([s00, s01], axis=1), q, (1, 0))
        dk_part[slot, hi] = dot(s11, q[hi], (1, 0))
        dq_own[h, :, lo] = dot(kt[:, lo], s00, (1, 0))
        dq_own[h, :, hi] = dot(kt, jnp.concatenate([s01, s11], axis=0), (1, 0))

    def shared(h):
        k, v, q, g = k_own[h], v_own[h], q_next[h], g_next[h]
        kt = k.T
        lse = stats_next[pl.ds(h, 1), :]
        delta = stats_next[pl.ds(heads + h, 1), :]

        def block(us, ts, number):
            return pair_block(k[us], v[us], q[ts], g[ts], lse[:, ts], delta[:, ts], number)

        p10, s10 = block(hi, lo, 3)
        p00, s00 = block(lo, lo, 4)
        p11, s11 = block(hi, hi, 5)
        dq_sent[h, :, lo] = dot(kt, jnp.concatenate([s00, s10], axis=0), (1, 0)).astype(
            jnp.bfloat16
        )
        dq_sent[h, :, hi] = dot(kt[:, hi], s11, (1, 0)).astype(jnp.bfloat16)
        slot = lax.rem(h, LEAD + 1)
        cols = columns(h)
        dv0 = dv_part[slot, lo] + dot(p00, g[lo], (1, 0))
        dv1 = dv_part[slot, hi] + dot(jnp.concatenate([p10, p11], axis=1), g, (1, 0))
        dk0 = dk_part[slot, lo] + dot(s00, q[lo], (1, 0))
        dk1 = dk_part[slot, hi] + dot(jnp.concatenate([s10, s11], axis=1), q, (1, 0))
        dv_out[lo, cols] = dv0.astype(jnp.bfloat16)
        dv_out[hi, cols] = dv1.astype(jnp.bfloat16)
        dk_out[lo, cols] = (dk0 * scale).astype(jnp.bfloat16)
        dk_out[hi, cols] = (dk1 * scale).astype(jnp.bfloat16)

    def finish(h):
        @pl.when(has_before)
        def _():
            to_after(h).wait_recv()

        total = (dq_own[h] + dq_got[h].astype(jnp.float32)) * scale
        dq_out[:, columns(h)] = total.T.astype(jnp.bfloat16)

    def lead(h, carry):
        head_load(h, 2).wait()
        head_load(h, 3).wait()
        local(h)
        return carry

    lax.fori_loop(0, LEAD, lead, 0)

    @pl.when(has_after)
    def _():
        stats_copy.wait_recv()

    @pl.when(jnp.logical_not(has_after))
    def _():
        stats_next[...] = jnp.full_like(stats_next, 2.0 * rows)

        def clear(h, carry):
            q_next[h] = jnp.zeros((rows, HEAD), jnp.bfloat16)
            g_next[h] = jnp.zeros((rows, HEAD), jnp.bfloat16)
            return carry

        lax.fori_loop(0, heads, clear, 0)

    @pl.when(jnp.logical_not(has_before))
    def _():
        def clear(h, carry):
            dq_got[h] = jnp.zeros((HEAD, rows), jnp.bfloat16)
            return carry

        lax.fori_loop(0, heads, clear, 0)

    bound = stats_next[2 * heads : 2 * heads + 1, :].astype(jnp.int32)
    bias[3] = hidden_where_not(key_at + half >= bound[:, lo])
    bias[4] = hidden_where_not(key_at >= bound[:, lo])
    bias[5] = hidden_where_not(key_at + half >= bound[:, hi])

    def step(h, more):
        if more:

            @pl.when(has_before)
            def _():
                for copy in to_before(h):
                    copy.wait_send()

            @pl.when(h + AHEAD < heads)
            def _():
                admit(h + AHEAD)

            head_load(h + LEAD, 2).wait()
            head_load(h + LEAD, 3).wait()

        @pl.when(has_after)
        def _():
            for copy in to_before(h):
                copy.wait_recv()

        shared(h)
        if more:
            local(h + LEAD)

        @pl.when(has_after)
        def _():
            to_after(h).start()

        @pl.when(h >= LAG)
        def _():
            finish(h - LAG)

    def both(h, carry):
        step(h, True)
        return carry

    def shared_only(h, carry):
        step(h, False)
        return carry

    lax.fori_loop(0, heads - LEAD, both, 0)
    lax.fori_loop(heads - LEAD, heads, shared_only, 0)
    lax.fori_loop(heads - LAG, heads, lambda h, c: (finish(h), c)[1], 0)

    def drain(h, carry):
        @pl.when(has_after)
        def _():
            to_after(h).wait_send()

        @pl.when(has_before & (h >= heads - LEAD))
        def _():
            for copy in to_before(h):
                copy.wait_send()

        return carry

    lax.fori_loop(0, heads, drain, 0)

    @pl.when(has_before)
    def _():
        stats_copy.wait_send()


def solution(mesh):
    groups, group_size = mesh.shape["grp"], mesh.shape["seq"]

    def local(q, k, v, o, g, lse, start, window):
        rows, model = q.shape
        heads = lse.shape[0]
        block = pltpu.VMEM((rows, model), jnp.bfloat16)
        per_head = pltpu.VMEM((heads, rows, HEAD), jnp.bfloat16)
        turned = pltpu.VMEM((heads, HEAD, rows), jnp.bfloat16)
        stats = pltpu.VMEM((2 * heads + 8, rows), jnp.float32)
        part = pltpu.VMEM((LEAD + 1, rows, HEAD), jnp.float32)
        return pl.pallas_call(
            functools.partial(kernel, groups, group_size, heads),
            out_shape=(block, block, block),
            in_specs=[pl.BlockSpec(memory_space=pl.ANY)] * 8,
            out_specs=(pl.BlockSpec(memory_space=pltpu.VMEM),) * 3,
            scratch_shapes=[
                per_head,
                per_head,
                per_head,
                per_head,
                block,
                block,
                pltpu.VMEM((heads, rows), jnp.float32),
                pltpu.VMEM((rows,), jnp.int32),
                pltpu.VMEM((rows,), jnp.int32),
                stats,
                stats,
                pltpu.VMEM((6, rows // 2, rows // 2), jnp.float32),
                per_head,
                per_head,
                part,
                part,
                pltpu.VMEM((heads, HEAD, rows), jnp.float32),
                turned,
                turned,
                pltpu.SemaphoreType.DMA((5,)),
                pltpu.SemaphoreType.DMA((4, heads)),
                pltpu.SemaphoreType.DMA((2, heads)),
                pltpu.SemaphoreType.DMA((2, heads)),
                pltpu.SemaphoreType.DMA((2,)),
                pltpu.SemaphoreType.DMA((heads,)),
                pltpu.SemaphoreType.DMA((heads,)),
            ],
            compiler_params=pltpu.CompilerParams(
                collective_id=0, has_side_effects=True, vmem_limit_bytes=48 * 2**20
            ),
        )(q, k, v, o, g, lse, start, window)

    block = P(("grp", "seq"), None)
    return jax.shard_map(
        local,
        mesh=mesh,
        in_specs=(block,) * 5 + (P(None, ("grp", "seq")),) + (P(("grp", "seq")),) * 2,
        out_specs=(block,) * 3,
        check_vma=False,
    )
```

```python
import functools

import jax
import jax.numpy as jnp
from jax import lax
from jax.experimental import pallas as pl
from jax.experimental.pallas import tpu as pltpu
from jax.sharding import PartitionSpec as P

MESH = pl.DeviceIdType.MESH
LOG2E = 1.4426950408889634
HEAD = 128
LEAD = 2
AHEAD = 3
LAG = 3
TURNED = 3
HIDDEN = -1e30


def dot(a, b, contract):
    return lax.dot_general(
        a, b, ((contract[:1], contract[1:]), ((), ())), preferred_element_type=jnp.float32
    )


def kernel(
    groups,
    group_size,
    heads,
    q_hbm,
    k_hbm,
    v_hbm,
    o_hbm,
    g_hbm,
    lse_hbm,
    start_hbm,
    window_hbm,
    dq_out,
    dk_out,
    dv_out,
    q_own,
    k_own,
    v_own,
    g_own,
    o_all,
    g_all,
    lse_own,
    start_own,
    window_own,
    stats_own,
    stats_next,
    bias,
    q_next,
    g_next,
    dk_part,
    dv_part,
    dq_own,
    dq_sent,
    dq_got,
    k_before,
    v_before,
    dk_sent,
    dv_sent,
    dk_got,
    dv_got,
    load_sem,
    head_sem,
    send_sem,
    recv_sem,
    stats_sem,
    back_send_sem,
    back_recv_sem,
    keys_send_sem,
    keys_recv_sem,
    grads_send_sem,
    grads_recv_sem,
):
    rows = q_hbm.shape[0]
    half = rows // 2
    count = groups * group_size
    here = lax.axis_index("grp") * group_size + lax.axis_index("seq")
    has_before, has_after = here > 0, here < count - 1
    scale = HEAD**-0.5
    lo, hi = slice(0, half), slice(half, rows)

    def place(index):
        return (index // group_size, lax.rem(index, group_size))

    before = place(lax.rem(here + count - 1, count))
    after = place(lax.rem(here + 1, count))

    def columns(h):
        return pl.ds(pl.multiple_of(h * HEAD, HEAD), HEAD)

    def head_load(h, number):
        source, target = ((q_hbm, q_own), (g_hbm, g_own), (k_hbm, k_own), (v_hbm, v_own))[number]
        return pltpu.make_async_copy(
            source.at[:, columns(h)], target.at[h], head_sem.at[number, h]
        )

    def to_before(h):
        return [
            pltpu.make_async_remote_copy(
                src_ref=source.at[h],
                dst_ref=target.at[h],
                send_sem=send_sem.at[number, h],
                recv_sem=recv_sem.at[number, h],
                device_id=before,
                device_id_type=MESH,
            )
            for number, (source, target) in enumerate(((q_own, q_next), (g_own, g_next)))
        ]

    def to_after(h):
        return pltpu.make_async_remote_copy(
            src_ref=dq_sent.at[h],
            dst_ref=dq_got.at[h],
            send_sem=back_send_sem.at[h],
            recv_sem=back_recv_sem.at[h],
            device_id=after,
            device_id_type=MESH,
        )

    def keys_to_after(h):
        return [
            pltpu.make_async_remote_copy(
                src_ref=source.at[h],
                dst_ref=target.at[h],
                send_sem=keys_send_sem.at[number, h],
                recv_sem=keys_recv_sem.at[number, h],
                device_id=after,
                device_id_type=MESH,
            )
            for number, (source, target) in enumerate(((k_own, k_before), (v_own, v_before)))
        ]

    def grads_to_before(h):
        return [
            pltpu.make_async_remote_copy(
                src_ref=source.at[h],
                dst_ref=target.at[h],
                send_sem=grads_send_sem.at[number, h],
                recv_sem=grads_recv_sem.at[number, h],
                device_id=before,
                device_id_type=MESH,
            )
            for number, (source, target) in enumerate(((dk_sent, dk_got), (dv_sent, dv_got)))
        ]

    stats_copy = pltpu.make_async_remote_copy(
        src_ref=stats_own,
        dst_ref=stats_next,
        send_sem=stats_sem.at[0],
        recv_sem=stats_sem.at[1],
        device_id=before,
        device_id_type=MESH,
    )

    whole_loads = [
        pltpu.make_async_copy(source, target, load_sem.at[number])
        for number, (source, target) in enumerate(
            (
                (o_hbm, o_all),
                (g_hbm, g_all),
                (lse_hbm, lse_own),
                (start_hbm, start_own),
                (window_hbm, window_own),
            )
        )
    ]
    barrier = pltpu.get_barrier_semaphore()
    for neighbour in (before, after):
        pl.semaphore_signal(barrier, inc=1, device_id=neighbour, device_id_type=MESH)

    head_load(TURNED, 0).start()
    head_load(TURNED, 1).start()
    for h in range(TURNED):
        head_load(h, 2).start()
        head_load(h, 3).start()
    for copy in whole_loads:
        copy.start()

    def start_loads(h, carry):
        for number in range(4):
            first = (h != TURNED) if number < 2 else (h >= TURNED)

            @pl.when(first)
            def _():
                head_load(h, number).start()

        return carry

    lax.fori_loop(0, heads, start_loads, 0)
    pl.semaphore_wait(barrier, 2)

    def admit(h):
        head_load(h, 0).wait()
        head_load(h, 1).wait()

        @pl.when(has_before)
        def _():
            for copy in to_before(h):
                copy.start()

    admit(TURNED)
    for h in range(TURNED):
        head_load(h, 2).wait()
        head_load(h, 3).wait()

        @pl.when(has_after)
        def _():
            for copy in keys_to_after(h):
                copy.start()


    for copy in whole_loads:
        copy.wait()
    positions = lax.broadcasted_iota(jnp.int32, (1, rows), 1)
    lowest = jnp.maximum(
        start_own[...].reshape(1, rows) - here * rows,
        positions - window_own[...].reshape(1, rows) + 1,
    )
    stats_own[0:heads, :] = lse_own[...] * LOG2E
    model = heads * HEAD
    picks = (
        lax.broadcasted_iota(jnp.int32, (heads, model), 1) // HEAD
        == lax.broadcasted_iota(jnp.int32, (heads, model), 0)
    ).astype(jnp.float32).astype(jnp.bfloat16)
    for r in range(0, rows, 128):
        products = o_all[r : r + 128, :].astype(jnp.float32) * g_all[r : r + 128, :].astype(
            jnp.float32
        )
        high = products.astype(jnp.bfloat16)
        low = (products - high.astype(jnp.float32)).astype(jnp.bfloat16)
        stats_own[heads : 2 * heads, r : r + 128] = dot(picks, high, (1, 1)) + dot(
            picks, low, (1, 1)
        )
    stats_own[2 * heads : 2 * heads + 8, :] = jnp.broadcast_to(
        (lowest + rows).astype(jnp.float32), (8, rows)
    )

    @pl.when(has_before)
    def _():
        stats_copy.start()

    for h in range(TURNED + 1, TURNED + AHEAD):
        admit(h)
    for h in range(TURNED):
        head_load(h, 0).wait()
        head_load(h, 1).wait()

    key_at = lax.broadcasted_iota(jnp.int32, (half, half), 0)
    query_at = lax.broadcasted_iota(jnp.int32, (half, half), 1)

    def hidden_where_not(mask):
        return jnp.where(mask, 0.0, HIDDEN)

    bias[0] = hidden_where_not((key_at >= lowest[:, lo]) & (key_at <= query_at))
    bias[1] = hidden_where_not(key_at >= lowest[:, hi])
    bias[2] = hidden_where_not((key_at + half >= lowest[:, hi]) & (key_at <= query_at))

    bias[6] = hidden_where_not(key_at - half >= lowest[:, lo])
    bias[7] = hidden_where_not(key_at - rows >= lowest[:, lo])
    bias[8] = hidden_where_not(key_at - half >= lowest[:, hi])

    def pair_block(k, v, q, g, lse, delta, number):
        s = dot(k, q, (1, 1)) * (scale * LOG2E) + bias[number]
        p = jnp.exp2(s - lse)
        ds = p * (dot(v, g, (1, 1)) - delta)
        return p.astype(jnp.bfloat16), ds.astype(jnp.bfloat16)

    def local(h):
        k, v, q, g = k_own[h], v_own[h], q_own[h], g_own[h]
        kt = k.T
        lse = stats_own[pl.ds(h, 1), :]
        delta = stats_own[pl.ds(heads + h, 1), :]

        def block(us, ts, number):
            return pair_block(k[us], v[us], q[ts], g[ts], lse[:, ts], delta[:, ts], number)

        p00, s00 = block(lo, lo, 0)
        p01, s01 = block(lo, hi, 1)
        p11, s11 = block(hi, hi, 2)
        slot = h
        dv_part[slot, lo] = dot(jnp.concatenate([p00, p01], axis=1), g, (1, 0))
        dv_part[slot, hi] = dot(p11, g[hi], (1, 0))
        dk_part[slot, lo] = dot(jnp.concatenate([s00, s01], axis=1), q, (1, 0))
        dk_part[slot, hi] = dot(s11, q[hi], (1, 0))
        dq_own[h, :, lo] = dot(kt[:, lo], s00, (1, 0))
        dq_own[h, :, hi] = dot(kt, jnp.concatenate([s01, s11], axis=0), (1, 0))

    def shared(h):
        k, v, q, g = k_own[h], v_own[h], q_next[h], g_next[h]
        kt = k.T
        lse = stats_next[pl.ds(h, 1), :]
        delta = stats_next[pl.ds(heads + h, 1), :]

        def block(us, ts, number):
            return pair_block(k[us], v[us], q[ts], g[ts], lse[:, ts], delta[:, ts], number)

        p10, s10 = block(hi, lo, 3)
        p00, s00 = block(lo, lo, 4)
        p11, s11 = block(hi, hi, 5)
        dq_sent[h, :, lo] = dot(kt, jnp.concatenate([s00, s10], axis=0), (1, 0)).astype(
            jnp.bfloat16
        )
        dq_sent[h, :, hi] = dot(kt[:, hi], s11, (1, 0)).astype(jnp.bfloat16)
        slot = h
        cols = columns(h)
        dv0 = dv_part[slot, lo] + dot(p00, g[lo], (1, 0))
        dv1 = dv_part[slot, hi] + dot(jnp.concatenate([p10, p11], axis=1), g, (1, 0))
        dk0 = dk_part[slot, lo] + dot(s00, q[lo], (1, 0))
        dk1 = dk_part[slot, hi] + dot(jnp.concatenate([s10, s11], axis=1), q, (1, 0))
        dv_out[lo, cols] = dv0.astype(jnp.bfloat16)
        dv_out[hi, cols] = dv1.astype(jnp.bfloat16)
        dk_out[lo, cols] = (dk0 * scale).astype(jnp.bfloat16)
        dk_out[hi, cols] = (dk1 * scale).astype(jnp.bfloat16)

    def turned(h):
        for copy in keys_to_after(h):
            copy.wait_recv()
        k, v, q, g = k_before[h], v_before[h], q_own[h], g_own[h]
        kt = k.T
        lse = stats_own[pl.ds(h, 1), :]
        delta = stats_own[pl.ds(heads + h, 1), :]

        def block(us, ts, number):
            return pair_block(k[us], v[us], q[ts], g[ts], lse[:, ts], delta[:, ts], number)

        p10, s10 = block(hi, lo, 6)
        p00, s00 = block(lo, lo, 7)
        p11, s11 = block(hi, hi, 8)
        dq_own[h, :, lo] += dot(kt, jnp.concatenate([s00, s10], axis=0), (1, 0))
        dq_own[h, :, hi] += dot(kt[:, hi], s11, (1, 0))
        dv0 = dot(p00, g[lo], (1, 0))
        dv1 = dot(jnp.concatenate([p10, p11], axis=1), g, (1, 0))
        dk0 = dot(s00, q[lo], (1, 0))
        dk1 = dot(jnp.concatenate([s10, s11], axis=1), q, (1, 0))
        dv_sent[h, lo] = dv0.astype(jnp.bfloat16)
        dv_sent[h, hi] = dv1.astype(jnp.bfloat16)
        dk_sent[h, lo] = dk0.astype(jnp.bfloat16)
        dk_sent[h, hi] = dk1.astype(jnp.bfloat16)

    def finish_turned(h):
        @pl.when(has_after)
        def _():
            for copy in grads_to_before(h):
                copy.wait_recv()
            dk_part[h] += dk_got[h].astype(jnp.float32)
            dv_part[h] += dv_got[h].astype(jnp.float32)

        dk_out[:, columns(h)] = (dk_part[h] * scale).astype(jnp.bfloat16)
        dv_out[:, columns(h)] = dv_part[h].astype(jnp.bfloat16)

    def finish(h):
        @pl.when(has_before)
        def _():
            to_after(h).wait_recv()

        total = (dq_own[h] + dq_got[h].astype(jnp.float32)) * scale
        dq_out[:, columns(h)] = total.T.astype(jnp.bfloat16)

    def lead(h, carry):
        @pl.when(h >= TURNED)
        def _():
            head_load(h, 2).wait()
            head_load(h, 3).wait()

        local(h)
        return carry

    lax.fori_loop(0, TURNED + LEAD, lead, 0)

    @pl.when(has_after)
    def _():
        stats_copy.wait_recv()

    @pl.when(jnp.logical_not(has_after))
    def _():
        stats_next[...] = jnp.full_like(stats_next, 2.0 * rows)

        def clear(h, carry):
            q_next[h] = jnp.zeros((rows, HEAD), jnp.bfloat16)
            g_next[h] = jnp.zeros((rows, HEAD), jnp.bfloat16)
            return carry

        lax.fori_loop(0, heads, clear, 0)

    @pl.when(jnp.logical_not(has_before))
    def _():
        def clear(h, carry):
            dq_got[h] = jnp.zeros((HEAD, rows), jnp.bfloat16)
            return carry

        lax.fori_loop(0, heads, clear, 0)

    bound = stats_next[2 * heads : 2 * heads + 1, :].astype(jnp.int32)
    bias[3] = hidden_where_not(key_at + half >= bound[:, lo])
    bias[4] = hidden_where_not(key_at >= bound[:, lo])
    bias[5] = hidden_where_not(key_at + half >= bound[:, hi])

    def step(h, more):
        if more:

            @pl.when(has_before)
            def _():
                for copy in to_before(h):
                    copy.wait_send()

            @pl.when(h + AHEAD < heads)
            def _():
                admit(h + AHEAD)

        else:

            @pl.when(has_before)
            def _():
                for copy in to_before(h):
                    copy.wait_send()

        @pl.when(has_before & (h + AHEAD >= heads))
        def _():
            for copy in grads_to_before(h + AHEAD - heads):
                copy.start()

        if more:
            head_load(h + LEAD, 2).wait()
            head_load(h + LEAD, 3).wait()

        @pl.when(has_after)
        def _():
            for copy in to_before(h):
                copy.wait_recv()

        shared(h)
        if more:
            local(h + LEAD)

        @pl.when(has_after)
        def _():
            to_after(h).start()

        @pl.when((h > TURNED) & (h <= 2 * TURNED))
        def _():
            @pl.when(has_before)
            def _():
                turned(h - TURNED - 1)

            dq_out[:, columns(h - TURNED - 1)] = (
                (dq_own[h - TURNED - 1] * scale).T.astype(jnp.bfloat16)
            )

        @pl.when(h >= TURNED + LAG)
        def _():
            finish(h - LAG)

    def both(h, carry):
        step(h, True)
        return carry

    def shared_only(h, carry):
        step(h, False)
        return carry

    lax.fori_loop(TURNED, heads - LEAD, both, 0)
    lax.fori_loop(heads - LEAD, heads, shared_only, 0)
    lax.fori_loop(heads - LAG, heads, lambda h, c: (finish(h), c)[1], 0)
    lax.fori_loop(0, TURNED, lambda h, c: (finish_turned(h), c)[1], 0)

    def drain(h, carry):
        @pl.when(has_after & (h >= TURNED))
        def _():
            to_after(h).wait_send()

        @pl.when(has_after & (h < TURNED))
        def _():
            for copy in keys_to_after(h):
                copy.wait_send()

        @pl.when(has_before & (h < TURNED))
        def _():
            for copy in grads_to_before(h):
                copy.wait_send()

        return carry

    lax.fori_loop(0, heads, drain, 0)

    @pl.when(has_before)
    def _():
        stats_copy.wait_send()


def write_out(*refs):
    sources, targets, sem = refs[:3], refs[3:6], refs[6]
    copies = [
        pltpu.make_async_copy(source, target, sem.at[number])
        for number, (source, target) in enumerate(zip(sources, targets))
    ]
    for copy in copies:
        copy.start()
    for copy in copies:
        copy.wait()


def solution(mesh):
    groups, group_size = mesh.shape["grp"], mesh.shape["seq"]

    def local(q, k, v, o, g, lse, start, window):
        rows, model = q.shape
        heads = lse.shape[0]
        block = pltpu.VMEM((rows, model), jnp.bfloat16)
        per_head = pltpu.VMEM((heads, rows, HEAD), jnp.bfloat16)
        turned = pltpu.VMEM((heads, HEAD, rows), jnp.bfloat16)
        stats = pltpu.VMEM((2 * heads + 8, rows), jnp.float32)
        part = pltpu.VMEM((heads, rows, HEAD), jnp.float32)
        few = pltpu.VMEM((TURNED, rows, HEAD), jnp.bfloat16)
        results = pl.pallas_call(
            functools.partial(kernel, groups, group_size, heads),
            out_shape=(block, block, block),
            in_specs=[pl.BlockSpec(memory_space=pl.ANY)] * 8,
            out_specs=(pl.BlockSpec(memory_space=pltpu.VMEM),) * 3,
            scratch_shapes=[
                per_head,
                per_head,
                per_head,
                per_head,
                block,
                block,
                pltpu.VMEM((heads, rows), jnp.float32),
                pltpu.VMEM((rows,), jnp.int32),
                pltpu.VMEM((rows,), jnp.int32),
                stats,
                stats,
                pltpu.VMEM((9, rows // 2, rows // 2), jnp.float32),
                per_head,
                per_head,
                part,
                part,
                pltpu.VMEM((heads, HEAD, rows), jnp.float32),
                turned,
                turned,
                few,
                few,
                few,
                few,
                few,
                few,
                pltpu.SemaphoreType.DMA((5,)),
                pltpu.SemaphoreType.DMA((4, heads)),
                pltpu.SemaphoreType.DMA((2, heads)),
                pltpu.SemaphoreType.DMA((2, heads)),
                pltpu.SemaphoreType.DMA((2,)),
                pltpu.SemaphoreType.DMA((heads,)),
                pltpu.SemaphoreType.DMA((heads,)),
                pltpu.SemaphoreType.DMA((2, TURNED)),
                pltpu.SemaphoreType.DMA((2, TURNED)),
                pltpu.SemaphoreType.DMA((2, TURNED)),
                pltpu.SemaphoreType.DMA((2, TURNED)),
            ],
            compiler_params=pltpu.CompilerParams(
                collective_id=0, has_side_effects=True, vmem_limit_bytes=48 * 2**20
            ),
        )(q, k, v, o, g, lse, start, window)
        return pl.pallas_call(
            write_out,
            out_shape=(jax.ShapeDtypeStruct((rows, model), jnp.bfloat16),) * 3,
            in_specs=[pl.BlockSpec(memory_space=pltpu.VMEM)] * 3,
            out_specs=(pl.BlockSpec(memory_space=pl.ANY),) * 3,
            scratch_shapes=[pltpu.SemaphoreType.DMA((3,))],
            compiler_params=pltpu.CompilerParams(vmem_limit_bytes=8 * 2**20),
        )(*(pltpu.with_memory_space_constraint(r, pltpu.VMEM) for r in results))

    block = P(("grp", "seq"), None)
    return jax.shard_map(
        local,
        mesh=mesh,
        in_specs=(block,) * 5 + (P(None, ("grp", "seq")),) + (P(("grp", "seq")),) * 2,
        out_specs=(block,) * 3,
        check_vma=False,
    )
```

```python
import functools

import jax
import jax.numpy as jnp
from jax import lax
from jax.experimental import pallas as pl
from jax.experimental.pallas import tpu as pltpu
from jax.sharding import PartitionSpec as P

MESH = pl.DeviceIdType.MESH
LOG2E = 1.4426950408889634
HEAD = 128
LEAD = 2
AHEAD = 3
LAG = 5
TURNED = 3
WRAPPED = 3
PLAIN = 1
FIRST = 5
LATE = 2
EARLY = 2
HIDDEN = -1e30


def dot(a, b, contract):
    return lax.dot_general(
        a, b, ((contract[:1], contract[1:]), ((), ())), preferred_element_type=jnp.float32
    )


def kernel(
    groups,
    group_size,
    heads,
    q_hbm,
    k_hbm,
    v_hbm,
    o_hbm,
    g_hbm,
    lse_hbm,
    start_hbm,
    window_hbm,
    dq_out,
    dk_out,
    dv_out,
    q_own,
    k_own,
    v_own,
    g_own,
    o_all,
    g_all,
    lse_own,
    start_own,
    window_own,
    stats_own,
    stats_next,
    bias,
    q_next,
    g_next,
    dk_part,
    dv_part,
    dq_own,
    dq_sent,
    dq_got,
    k_before,
    v_before,
    dk_sent,
    dv_sent,
    dk_got,
    dv_got,
    q_relay,
    g_relay,
    load_sem,
    head_sem,
    send_sem,
    recv_sem,
    stats_sem,
    back_send_sem,
    back_recv_sem,
    keys_send_sem,
    keys_recv_sem,
    grads_send_sem,
    grads_recv_sem,
    relay_send_sem,
    relay_recv_sem,
    forward_send_sem,
    ready_sem,
):
    rows = q_hbm.shape[0]
    half = rows // 2
    count = groups * group_size
    here = lax.axis_index("grp") * group_size + lax.axis_index("seq")
    has_before, has_after = here > 0, here < count - 1
    scale = HEAD**-0.5
    lo, hi = slice(0, half), slice(half, rows)

    def place(index):
        return (index // group_size, lax.rem(index, group_size))

    before = place(lax.rem(here + count - 1, count))
    after = place(lax.rem(here + 1, count))

    core = lax.rem(here, 2)
    z = lax.rem(here // 2, 4)
    ring = here - 2 * z - core
    even_z = lax.rem(z, 2) == 0
    detours = (core == 0) & has_before
    detoured = jnp.where(detours, jnp.where(z == 0, WRAPPED, PLAIN), 0)
    direct = heads - TURNED - detoured
    leaves = heads - LATE
    relay_of_here = place(ring + 2 * lax.rem(z + jnp.where(even_z, 2, 1), 4) + 1)
    relays = (core == 1) & even_z
    first_client = ring + 2 * lax.rem(z + 2, 4)
    second_client = ring + 2 * lax.rem(z + 3, 4)
    relays_first = relays & (first_client > 0)
    first_count = jnp.where(z == 2, WRAPPED, PLAIN)
    next_z = lax.rem(z + 1, 4)
    next_ring = here + 1 - 2 * next_z
    relay_of_after = place(next_ring + 2 * lax.rem(next_z + jnp.where(even_z, 1, 2), 4) + 1)

    def columns(h):
        return pl.ds(pl.multiple_of(h * HEAD, HEAD), HEAD)

    def head_load(h, number):
        source, target = ((q_hbm, q_own), (g_hbm, g_own), (k_hbm, k_own), (v_hbm, v_own))[number]
        return pltpu.make_async_copy(
            source.at[:, columns(h)], target.at[h], head_sem.at[number, h]
        )

    def to_before(h):
        return [
            pltpu.make_async_remote_copy(
                src_ref=source.at[h],
                dst_ref=target.at[h],
                send_sem=send_sem.at[number, h],
                recv_sem=recv_sem.at[number, h],
                device_id=before,
                device_id_type=MESH,
            )
            for number, (source, target) in enumerate(((q_own, q_next), (g_own, g_next)))
        ]

    def to_after(h):
        return pltpu.make_async_remote_copy(
            src_ref=dq_sent.at[h],
            dst_ref=dq_got.at[h],
            send_sem=back_send_sem.at[h],
            recv_sem=back_recv_sem.at[h],
            device_id=after,
            device_id_type=MESH,
        )

    def keys_to_after(h):
        return [
            pltpu.make_async_remote_copy(
                src_ref=source.at[h],
                dst_ref=target.at[h],
                send_sem=keys_send_sem.at[number, h],
                recv_sem=keys_recv_sem.at[number, h],
                device_id=after,
                device_id_type=MESH,
            )
            for number, (source, target) in enumerate(((k_own, k_before), (v_own, v_before)))
        ]

    def grads_to_before(h):
        return [
            pltpu.make_async_remote_copy(
                src_ref=source.at[h],
                dst_ref=target.at[h],
                send_sem=grads_send_sem.at[number, h],
                recv_sem=grads_recv_sem.at[number, h],
                device_id=before,
                device_id_type=MESH,
            )
            for number, (source, target) in enumerate(((dk_sent, dk_got), (dv_sent, dv_got)))
        ]

    def to_relay(h):
        slot = h - (leaves - detoured) + jnp.where(even_z, 0, WRAPPED)
        return [
            pltpu.make_async_remote_copy(
                src_ref=source.at[h],
                dst_ref=target.at[slot],
                send_sem=relay_send_sem.at[number, slot],
                recv_sem=relay_recv_sem.at[number, slot],
                device_id=relay_of_here,
                device_id_type=MESH,
            )
            for number, (source, target) in enumerate(((q_own, q_relay), (g_own, g_relay)))
        ]

    def forward(slot, h, client):
        return [
            pltpu.make_async_remote_copy(
                src_ref=source.at[slot],
                dst_ref=target.at[h],
                send_sem=forward_send_sem.at[number, slot],
                recv_sem=recv_sem.at[number, h],
                device_id=place(client - 1),
                device_id_type=MESH,
            )
            for number, (source, target) in enumerate(((q_relay, q_next), (g_relay, g_next)))
        ]

    def forwards(slot):
        if slot < WRAPPED:
            wanted = relays_first & (slot < first_count)
            return wanted, forward(slot, leaves - first_count + slot, first_client)
        return relays, forward(slot, leaves - PLAIN + slot - WRAPPED, second_client)

    def arrived(slot):
        return [
            pltpu.make_async_remote_copy(
                src_ref=source.at[0],
                dst_ref=target.at[slot],
                send_sem=relay_send_sem.at[number, slot],
                recv_sem=relay_recv_sem.at[number, slot],
                device_id=before,
                device_id_type=MESH,
            )
            for number, (source, target) in enumerate(((q_own, q_relay), (g_own, g_relay)))
        ]

    stats_copy = pltpu.make_async_remote_copy(
        src_ref=stats_own,
        dst_ref=stats_next,
        send_sem=stats_sem.at[0],
        recv_sem=stats_sem.at[1],
        device_id=before,
        device_id_type=MESH,
    )

    whole_loads = [
        pltpu.make_async_copy(source, target, load_sem.at[number])
        for number, (source, target) in enumerate(
            (
                (o_hbm, o_all),
                (g_hbm, g_all),
                (lse_hbm, lse_own),
                (start_hbm, start_own),
                (window_hbm, window_own),
            )
        )
    ]
    barrier = pltpu.get_barrier_semaphore()

    def greet(wanted, device):
        @pl.when(wanted)
        def _():
            pl.semaphore_signal(barrier, inc=1, device_id=device, device_id_type=MESH)

    greet(has_after, after)
    greet(has_before, before)
    greet(detours, relay_of_here)
    greet((core == 1) & has_after, relay_of_after)

    for h in range(TURNED, TURNED + EARLY):
        head_load(h, 0).start()
        head_load(h, 1).start()
    for h in range(TURNED):
        head_load(h, 2).start()
        head_load(h, 3).start()
    for copy in whole_loads:
        copy.start()

    def start_loads(h, carry):
        for number in range(4):
            first = ((h < TURNED) | (h >= TURNED + EARLY)) if number < 2 else (h >= TURNED)

            @pl.when(first)
            def _():
                head_load(h, number).start()

        return carry

    lax.fori_loop(0, heads, start_loads, 0)
    pl.semaphore_wait(
        barrier,
        has_before.astype(jnp.int32)
        + has_after.astype(jnp.int32)
        + 2 * relays.astype(jnp.int32)
        + 2 * relays_first.astype(jnp.int32),
    )

    @pl.when(relays_first)
    def _():
        pl.semaphore_signal(
            ready_sem, inc=1, device_id=place(first_client), device_id_type=MESH
        )

    @pl.when(relays)
    def _():
        pl.semaphore_signal(
            ready_sem, inc=1, device_id=place(second_client), device_id_type=MESH
        )

    def direct_head(item):
        h = TURNED + item
        return jnp.where(h < leaves - detoured, h, h + detoured)

    def admit(h):
        @pl.when(has_before)
        def _():
            for copy in to_before(h):
                copy.start()

    for h in range(TURNED, TURNED + EARLY):
        head_load(h, 0).wait()
        head_load(h, 1).wait()
        admit(h)
    for h in range(TURNED):
        head_load(h, 2).wait()
        head_load(h, 3).wait()

        @pl.when(has_after)
        def _():
            for copy in keys_to_after(h):
                copy.start()


    for copy in whole_loads:
        copy.wait()
    positions = lax.broadcasted_iota(jnp.int32, (1, rows), 1)
    lowest = jnp.maximum(
        start_own[...].reshape(1, rows) - here * rows,
        positions - window_own[...].reshape(1, rows) + 1,
    )
    stats_own[0:heads, :] = lse_own[...] * LOG2E
    model = heads * HEAD
    picks = (
        lax.broadcasted_iota(jnp.int32, (heads, model), 1) // HEAD
        == lax.broadcasted_iota(jnp.int32, (heads, model), 0)
    ).astype(jnp.float32).astype(jnp.bfloat16)
    for r in range(0, rows, 128):
        products = o_all[r : r + 128, :].astype(jnp.float32) * g_all[r : r + 128, :].astype(
            jnp.float32
        )
        high = products.astype(jnp.bfloat16)
        low = (products - high.astype(jnp.float32)).astype(jnp.bfloat16)
        stats_own[heads : 2 * heads, r : r + 128] = dot(picks, high, (1, 1)) + dot(
            picks, low, (1, 1)
        )
    stats_own[2 * heads : 2 * heads + 8, :] = jnp.broadcast_to(
        (lowest + rows).astype(jnp.float32), (8, rows)
    )

    @pl.when(has_before)
    def _():
        stats_copy.start()

    def settle(h, carry):
        for number in range(4):
            waits = ((h < TURNED) | (h >= TURNED + EARLY)) if number < 2 else (h >= TURNED)

            @pl.when(waits)
            def _():
                head_load(h, number).wait()

        return carry

    lax.fori_loop(0, heads, settle, 0)
    for h in range(TURNED + EARLY, TURNED + AHEAD):
        admit(h)

    key_at = lax.broadcasted_iota(jnp.int32, (half, half), 0)
    query_at = lax.broadcasted_iota(jnp.int32, (half, half), 1)

    def hidden_where_not(mask):
        return jnp.where(mask, 0.0, HIDDEN)

    bias[0] = hidden_where_not((key_at >= lowest[:, lo]) & (key_at <= query_at))
    bias[1] = hidden_where_not(key_at >= lowest[:, hi])
    bias[2] = hidden_where_not((key_at + half >= lowest[:, hi]) & (key_at <= query_at))

    bias[6] = hidden_where_not(key_at - half >= lowest[:, lo])
    bias[7] = hidden_where_not(key_at - rows >= lowest[:, lo])
    bias[8] = hidden_where_not(key_at - half >= lowest[:, hi])

    def pair_block(k, v, q, g, lse, delta, number):
        s = dot(k, q, (1, 1)) * (scale * LOG2E) + bias[number]
        p = jnp.exp2(s - lse)
        ds = p * (dot(v, g, (1, 1)) - delta)
        return p.astype(jnp.bfloat16), ds.astype(jnp.bfloat16)

    def local(h):
        k, v, q, g = k_own[h], v_own[h], q_own[h], g_own[h]
        kt = k.T
        lse = stats_own[pl.ds(h, 1), :]
        delta = stats_own[pl.ds(heads + h, 1), :]

        def block(us, ts, number):
            return pair_block(k[us], v[us], q[ts], g[ts], lse[:, ts], delta[:, ts], number)

        p00, s00 = block(lo, lo, 0)
        p01, s01 = block(lo, hi, 1)
        p11, s11 = block(hi, hi, 2)
        slot = h
        dv_part[slot, lo] = dot(jnp.concatenate([p00, p01], axis=1), g, (1, 0))
        dv_part[slot, hi] = dot(p11, g[hi], (1, 0))
        dk_part[slot, lo] = dot(jnp.concatenate([s00, s01], axis=1), q, (1, 0))
        dk_part[slot, hi] = dot(s11, q[hi], (1, 0))
        dq_own[h, :, lo] = dot(kt[:, lo], s00, (1, 0))
        dq_own[h, :, hi] = dot(kt, jnp.concatenate([s01, s11], axis=0), (1, 0))

    def shared(h):
        k, v, q, g = k_own[h], v_own[h], q_next[h], g_next[h]
        kt = k.T
        lse = stats_next[pl.ds(h, 1), :]
        delta = stats_next[pl.ds(heads + h, 1), :]

        def block(us, ts, number):
            return pair_block(k[us], v[us], q[ts], g[ts], lse[:, ts], delta[:, ts], number)

        p10, s10 = block(hi, lo, 3)
        p00, s00 = block(lo, lo, 4)
        p11, s11 = block(hi, hi, 5)
        dq_sent[h, :, lo] = dot(kt, jnp.concatenate([s00, s10], axis=0), (1, 0)).astype(
            jnp.bfloat16
        )
        dq_sent[h, :, hi] = dot(kt[:, hi], s11, (1, 0)).astype(jnp.bfloat16)
        slot = h
        cols = columns(h)
        dv0 = dv_part[slot, lo] + dot(p00, g[lo], (1, 0))
        dv1 = dv_part[slot, hi] + dot(jnp.concatenate([p10, p11], axis=1), g, (1, 0))
        dk0 = dk_part[slot, lo] + dot(s00, q[lo], (1, 0))
        dk1 = dk_part[slot, hi] + dot(jnp.concatenate([s10, s11], axis=1), q, (1, 0))
        dv_out[lo, cols] = dv0.astype(jnp.bfloat16)
        dv_out[hi, cols] = dv1.astype(jnp.bfloat16)
        dk_out[lo, cols] = (dk0 * scale).astype(jnp.bfloat16)
        dk_out[hi, cols] = (dk1 * scale).astype(jnp.bfloat16)

    def turned(h):
        for copy in keys_to_after(h):
            copy.wait_recv()
        k, v, q, g = k_before[h], v_before[h], q_own[h], g_own[h]
        kt = k.T
        lse = stats_own[pl.ds(h, 1), :]
        delta = stats_own[pl.ds(heads + h, 1), :]

        def block(us, ts, number):
            return pair_block(k[us], v[us], q[ts], g[ts], lse[:, ts], delta[:, ts], number)

        p10, s10 = block(hi, lo, 6)
        p00, s00 = block(lo, lo, 7)
        p11, s11 = block(hi, hi, 8)
        dq_own[h, :, lo] += dot(kt, jnp.concatenate([s00, s10], axis=0), (1, 0))
        dq_own[h, :, hi] += dot(kt[:, hi], s11, (1, 0))
        dv0 = dot(p00, g[lo], (1, 0))
        dv1 = dot(jnp.concatenate([p10, p11], axis=1), g, (1, 0))
        dk0 = dot(s00, q[lo], (1, 0))
        dk1 = dot(jnp.concatenate([s10, s11], axis=1), q, (1, 0))
        dv_sent[h, lo] = dv0.astype(jnp.bfloat16)
        dv_sent[h, hi] = dv1.astype(jnp.bfloat16)
        dk_sent[h, lo] = dk0.astype(jnp.bfloat16)
        dk_sent[h, hi] = dk1.astype(jnp.bfloat16)

    def finish_turned(h):
        @pl.when(has_after)
        def _():
            for copy in grads_to_before(h):
                copy.wait_recv()
            dk_part[h] += dk_got[h].astype(jnp.float32)
            dv_part[h] += dv_got[h].astype(jnp.float32)

        dk_out[:, columns(h)] = (dk_part[h] * scale).astype(jnp.bfloat16)
        dv_out[:, columns(h)] = dv_part[h].astype(jnp.bfloat16)

    def finish(h):
        @pl.when(has_before)
        def _():
            to_after(h).wait_recv()

        total = (dq_own[h] + dq_got[h].astype(jnp.float32)) * scale
        dq_out[:, columns(h)] = total.T.astype(jnp.bfloat16)

    def lead(h, carry):
        local(h)
        return carry

    lax.fori_loop(0, TURNED + LEAD, lead, 0)

    @pl.when(detours)
    def _():
        pl.semaphore_wait(ready_sem, 1)

        def leave(h, carry):
            for copy in to_relay(h):
                copy.start()
            return carry

        lax.fori_loop(leaves - detoured, leaves, leave, 0)


    @pl.when(has_after)
    def _():
        stats_copy.wait_recv()

    @pl.when(jnp.logical_not(has_after))
    def _():
        stats_next[...] = jnp.full_like(stats_next, 2.0 * rows)

        def clear(h, carry):
            q_next[h] = jnp.zeros((rows, HEAD), jnp.bfloat16)
            g_next[h] = jnp.zeros((rows, HEAD), jnp.bfloat16)
            return carry

        lax.fori_loop(0, heads, clear, 0)

    @pl.when(jnp.logical_not(has_before))
    def _():
        def clear(h, carry):
            dq_got[h] = jnp.zeros((HEAD, rows), jnp.bfloat16)
            return carry

        lax.fori_loop(0, heads, clear, 0)

    bound = stats_next[2 * heads : 2 * heads + 1, :].astype(jnp.int32)
    bias[3] = hidden_where_not(key_at + half >= bound[:, lo])
    bias[4] = hidden_where_not(key_at >= bound[:, lo])
    bias[5] = hidden_where_not(key_at + half >= bound[:, hi])

    def step(h, more):
        item = h - TURNED

        @pl.when(has_before & (item < direct))
        def _():
            for copy in to_before(direct_head(item)):
                copy.wait_send()

        @pl.when(item + AHEAD < direct)
        def _():
            admit(direct_head(item + AHEAD))

        @pl.when(has_before & (item + AHEAD >= direct) & (item + AHEAD < direct + TURNED))
        def _():
            for copy in grads_to_before(item + AHEAD - direct):
                copy.start()

        for slot in range(WRAPPED + PLAIN):
            wanted, copies = forwards(slot)

            @pl.when(wanted & (h == TURNED + FIRST + (slot + PLAIN) % (WRAPPED + PLAIN)))
            def _():
                for copy in arrived(slot):
                    copy.wait_recv()
                for copy in copies:
                    copy.start()

        @pl.when(has_after)
        def _():
            for copy in to_before(h):
                copy.wait_recv()

        shared(h)
        if more:
            local(h + LEAD)

        @pl.when(has_after)
        def _():
            to_after(h).start()

        @pl.when((h > TURNED) & (h <= 2 * TURNED))
        def _():
            @pl.when(has_before)
            def _():
                turned(h - TURNED - 1)

            dq_out[:, columns(h - TURNED - 1)] = (
                (dq_own[h - TURNED - 1] * scale).T.astype(jnp.bfloat16)
            )

        @pl.when(h >= TURNED + LAG)
        def _():
            finish(h - LAG)

    def both(h, carry):
        step(h, True)
        return carry

    def shared_only(h, carry):
        step(h, False)
        return carry

    lax.fori_loop(TURNED, heads - LEAD, both, 0)
    lax.fori_loop(heads - LEAD, heads, shared_only, 0)
    lax.fori_loop(heads - LAG, heads, lambda h, c: (finish(h), c)[1], 0)
    lax.fori_loop(0, TURNED, lambda h, c: (finish_turned(h), c)[1], 0)

    def drain(h, carry):
        @pl.when(has_after & (h >= TURNED))
        def _():
            to_after(h).wait_send()

        @pl.when(has_after & (h < TURNED))
        def _():
            for copy in keys_to_after(h):
                copy.wait_send()

        @pl.when(has_before & (h < TURNED))
        def _():
            for copy in grads_to_before(h):
                copy.wait_send()

        return carry

    lax.fori_loop(0, heads, drain, 0)

    @pl.when(detours)
    def _():
        def left(h, carry):
            for copy in to_relay(h):
                copy.wait_send()
            return carry

        lax.fori_loop(leaves - detoured, leaves, left, 0)

    for slot in range(WRAPPED + PLAIN):
        wanted, copies = forwards(slot)

        @pl.when(wanted)
        def _():
            for copy in copies:
                copy.wait_send()

    @pl.when(has_before)
    def _():
        stats_copy.wait_send()


def write_out(*refs):
    sources, targets, sem = refs[:3], refs[3:6], refs[6]
    copies = [
        pltpu.make_async_copy(source, target, sem.at[number])
        for number, (source, target) in enumerate(zip(sources, targets))
    ]
    for copy in copies:
        copy.start()
    for copy in copies:
        copy.wait()


def solution(mesh):
    groups, group_size = mesh.shape["grp"], mesh.shape["seq"]

    def local(q, k, v, o, g, lse, start, window):
        rows, model = q.shape
        heads = lse.shape[0]
        block = pltpu.VMEM((rows, model), jnp.bfloat16)
        per_head = pltpu.VMEM((heads, rows, HEAD), jnp.bfloat16)
        turned = pltpu.VMEM((heads, HEAD, rows), jnp.bfloat16)
        stats = pltpu.VMEM((2 * heads + 8, rows), jnp.float32)
        part = pltpu.VMEM((heads, rows, HEAD), jnp.float32)
        few = pltpu.VMEM((TURNED, rows, HEAD), jnp.bfloat16)
        relay = pltpu.VMEM((WRAPPED + PLAIN, rows, HEAD), jnp.bfloat16)
        results = pl.pallas_call(
            functools.partial(kernel, groups, group_size, heads),
            out_shape=(block, block, block),
            in_specs=[pl.BlockSpec(memory_space=pl.ANY)] * 8,
            out_specs=(pl.BlockSpec(memory_space=pltpu.VMEM),) * 3,
            scratch_shapes=[
                per_head,
                per_head,
                per_head,
                per_head,
                block,
                block,
                pltpu.VMEM((heads, rows), jnp.float32),
                pltpu.VMEM((rows,), jnp.int32),
                pltpu.VMEM((rows,), jnp.int32),
                stats,
                stats,
                pltpu.VMEM((9, rows // 2, rows // 2), jnp.float32),
                per_head,
                per_head,
                part,
                part,
                pltpu.VMEM((heads, HEAD, rows), jnp.float32),
                turned,
                turned,
                few,
                few,
                few,
                few,
                few,
                few,
                relay,
                relay,
                pltpu.SemaphoreType.DMA((5,)),
                pltpu.SemaphoreType.DMA((4, heads)),
                pltpu.SemaphoreType.DMA((2, heads)),
                pltpu.SemaphoreType.DMA((2, heads)),
                pltpu.SemaphoreType.DMA((2,)),
                pltpu.SemaphoreType.DMA((heads,)),
                pltpu.SemaphoreType.DMA((heads,)),
                pltpu.SemaphoreType.DMA((2, TURNED)),
                pltpu.SemaphoreType.DMA((2, TURNED)),
                pltpu.SemaphoreType.DMA((2, TURNED)),
                pltpu.SemaphoreType.DMA((2, TURNED)),
                pltpu.SemaphoreType.DMA((2, WRAPPED + PLAIN)),
                pltpu.SemaphoreType.DMA((2, WRAPPED + PLAIN)),
                pltpu.SemaphoreType.DMA((2, WRAPPED + PLAIN)),
                pltpu.SemaphoreType.REGULAR,
            ],
            compiler_params=pltpu.CompilerParams(
                collective_id=0, has_side_effects=True, vmem_limit_bytes=48 * 2**20
            ),
        )(q, k, v, o, g, lse, start, window)
        return pl.pallas_call(
            write_out,
            out_shape=(jax.ShapeDtypeStruct((rows, model), jnp.bfloat16),) * 3,
            in_specs=[pl.BlockSpec(memory_space=pltpu.VMEM)] * 3,
            out_specs=(pl.BlockSpec(memory_space=pl.ANY),) * 3,
            scratch_shapes=[pltpu.SemaphoreType.DMA((3,))],
            compiler_params=pltpu.CompilerParams(vmem_limit_bytes=8 * 2**20),
        )(*(pltpu.with_memory_space_constraint(r, pltpu.VMEM) for r in results))

    block = P(("grp", "seq"), None)
    return jax.shard_map(
        local,
        mesh=mesh,
        in_specs=(block,) * 5 + (P(None, ("grp", "seq")),) + (P(("grp", "seq")),) * 2,
        out_specs=(block,) * 3,
        check_vma=False,
    )
```

```python
import functools

import jax
import jax.numpy as jnp
from jax import lax
from jax.experimental import pallas as pl
from jax.experimental.pallas import tpu as pltpu
from jax.sharding import PartitionSpec as P

MESH = pl.DeviceIdType.MESH
LOG2E = 1.4426950408889634
HEAD = 128
LEAD = 2
AHEAD = 4
LAG = 9
TURNED = 3
WRAPPED = 3
PLAIN = 1
PACE = 2
FORWARDED = (4, 6, 8, 2)
LATE = 2
EARLY = 3
HIDDEN = -1e30


def dot(a, b, contract):
    return lax.dot_general(
        a, b, ((contract[:1], contract[1:]), ((), ())), preferred_element_type=jnp.float32
    )


def kernel(
    groups,
    group_size,
    heads,
    q_hbm,
    k_hbm,
    v_hbm,
    o_hbm,
    g_hbm,
    lse_hbm,
    start_hbm,
    window_hbm,
    dq_out,
    dk_out,
    dv_out,
    q_own,
    k_own,
    v_own,
    g_own,
    o_all,
    g_all,
    lse_own,
    start_own,
    window_own,
    stats_own,
    stats_next,
    bias,
    q_next,
    g_next,
    dk_part,
    dv_part,
    dq_own,
    dq_sent,
    dq_got,
    k_before,
    v_before,
    dk_sent,
    dv_sent,
    dk_got,
    dv_got,
    q_relay,
    g_relay,
    load_sem,
    head_sem,
    send_sem,
    recv_sem,
    stats_sem,
    back_send_sem,
    back_recv_sem,
    keys_send_sem,
    keys_recv_sem,
    grads_send_sem,
    grads_recv_sem,
    relay_send_sem,
    relay_recv_sem,
    forward_send_sem,
    ready_sem,
):
    rows = q_hbm.shape[0]
    half = rows // 2
    count = groups * group_size
    here = lax.axis_index("grp") * group_size + lax.axis_index("seq")
    has_before, has_after = here > 0, here < count - 1
    scale = HEAD**-0.5
    lo, hi = slice(0, half), slice(half, rows)

    def place(index):
        return (index // group_size, lax.rem(index, group_size))

    before = place(lax.rem(here + count - 1, count))
    after = place(lax.rem(here + 1, count))

    core = lax.rem(here, 2)
    z = lax.rem(here // 2, 4)
    ring = here - 2 * z - core
    even_z = lax.rem(z, 2) == 0
    detours = (core == 0) & has_before
    detoured = jnp.where(detours, jnp.where(z == 0, WRAPPED, PLAIN), 0)
    direct = heads - TURNED - detoured
    leaves = heads - LATE
    relay_of_here = place(ring + 2 * lax.rem(z + jnp.where(even_z, 2, 1), 4) + 1)
    relays = (core == 1) & even_z
    first_client = ring + 2 * lax.rem(z + 2, 4)
    second_client = ring + 2 * lax.rem(z + 3, 4)
    relays_first = relays & (first_client > 0)
    first_count = jnp.where(z == 2, WRAPPED, PLAIN)
    next_z = lax.rem(z + 1, 4)
    next_ring = here + 1 - 2 * next_z
    relay_of_after = place(next_ring + 2 * lax.rem(next_z + jnp.where(even_z, 1, 2), 4) + 1)

    def columns(h):
        return pl.ds(pl.multiple_of(h * HEAD, HEAD), HEAD)

    def head_load(h, number):
        source, target = ((q_hbm, q_own), (g_hbm, g_own), (k_hbm, k_own), (v_hbm, v_own))[number]
        return pltpu.make_async_copy(
            source.at[:, columns(h)], target.at[h], head_sem.at[number, h]
        )

    def to_before(h, early=False):
        return [
            pltpu.make_async_remote_copy(
                src_ref=origin.at[:, columns(h)] if early else source.at[h],
                dst_ref=target.at[h],
                send_sem=send_sem.at[number, h],
                recv_sem=recv_sem.at[number, h],
                device_id=before,
                device_id_type=MESH,
            )
            for number, (origin, source, target) in enumerate(
                ((q_hbm, q_own, q_next), (g_hbm, g_own, g_next))
            )
        ]

    def to_after(h):
        return pltpu.make_async_remote_copy(
            src_ref=dq_sent.at[h],
            dst_ref=dq_got.at[h],
            send_sem=back_send_sem.at[h],
            recv_sem=back_recv_sem.at[h],
            device_id=after,
            device_id_type=MESH,
        )

    def keys_to_after(h):
        return [
            pltpu.make_async_remote_copy(
                src_ref=source.at[:, columns(h)],
                dst_ref=target.at[h],
                send_sem=keys_send_sem.at[number, h],
                recv_sem=keys_recv_sem.at[number, h],
                device_id=after,
                device_id_type=MESH,
            )
            for number, (source, target) in enumerate(((k_hbm, k_before), (v_hbm, v_before)))
        ]

    def grads_to_before(h):
        return [
            pltpu.make_async_remote_copy(
                src_ref=source.at[h],
                dst_ref=target.at[h],
                send_sem=grads_send_sem.at[number, h],
                recv_sem=grads_recv_sem.at[number, h],
                device_id=before,
                device_id_type=MESH,
            )
            for number, (source, target) in enumerate(((dk_sent, dk_got), (dv_sent, dv_got)))
        ]

    def to_relay(h):
        slot = h - (leaves - detoured) + jnp.where(even_z, 0, WRAPPED)
        return [
            pltpu.make_async_remote_copy(
                src_ref=source.at[h],
                dst_ref=target.at[slot],
                send_sem=relay_send_sem.at[number, slot],
                recv_sem=relay_recv_sem.at[number, slot],
                device_id=relay_of_here,
                device_id_type=MESH,
            )
            for number, (source, target) in enumerate(((q_own, q_relay), (g_own, g_relay)))
        ]

    def forward(slot, h, client):
        return [
            pltpu.make_async_remote_copy(
                src_ref=source.at[slot],
                dst_ref=target.at[h],
                send_sem=forward_send_sem.at[number, slot],
                recv_sem=recv_sem.at[number, h],
                device_id=place(client - 1),
                device_id_type=MESH,
            )
            for number, (source, target) in enumerate(((q_relay, q_next), (g_relay, g_next)))
        ]

    def forwards(slot):
        if slot < WRAPPED:
            wanted = relays_first & (slot < first_count)
            return wanted, forward(slot, leaves - first_count + slot, first_client)
        return relays, forward(slot, leaves - PLAIN + slot - WRAPPED, second_client)

    def arrived(slot):
        return [
            pltpu.make_async_remote_copy(
                src_ref=source.at[0],
                dst_ref=target.at[slot],
                send_sem=relay_send_sem.at[number, slot],
                recv_sem=relay_recv_sem.at[number, slot],
                device_id=before,
                device_id_type=MESH,
            )
            for number, (source, target) in enumerate(((q_own, q_relay), (g_own, g_relay)))
        ]

    stats_copy = pltpu.make_async_remote_copy(
        src_ref=stats_own,
        dst_ref=stats_next,
        send_sem=stats_sem.at[0],
        recv_sem=stats_sem.at[1],
        device_id=before,
        device_id_type=MESH,
    )

    whole_loads = [
        pltpu.make_async_copy(source, target, load_sem.at[number])
        for number, (source, target) in enumerate(
            (
                (o_hbm, o_all),
                (g_hbm, g_all),
                (lse_hbm, lse_own),
                (start_hbm, start_own),
                (window_hbm, window_own),
            )
        )
    ]
    barrier = pltpu.get_barrier_semaphore()

    def greet(wanted, device):
        @pl.when(wanted)
        def _():
            pl.semaphore_signal(barrier, inc=1, device_id=device, device_id_type=MESH)

    greet(has_after, after)
    greet(has_before, before)
    greet(detours, relay_of_here)
    greet((core == 1) & has_after, relay_of_after)

    for copy in whole_loads:
        copy.start()

    pl.semaphore_wait(
        barrier,
        has_before.astype(jnp.int32)
        + has_after.astype(jnp.int32)
        + 2 * relays.astype(jnp.int32)
        + 2 * relays_first.astype(jnp.int32),
    )

    @pl.when(relays_first)
    def _():
        pl.semaphore_signal(
            ready_sem, inc=1, device_id=place(first_client), device_id_type=MESH
        )

    @pl.when(relays)
    def _():
        pl.semaphore_signal(
            ready_sem, inc=1, device_id=place(second_client), device_id_type=MESH
        )

    def direct_head(item):
        h = TURNED + item
        return jnp.where(h < leaves - detoured, h, h + detoured)

    def admit(h, early=False):
        @pl.when(has_before)
        def _():
            for copy in to_before(h, early):
                copy.start()

    for h in range(TURNED, TURNED + EARLY):
        admit(h, True)

    @pl.when(has_after)
    def _():
        for h in range(TURNED):
            for copy in keys_to_after(h):
                copy.start()

    def start_loads(h, carry):
        for number in range(4):
            head_load(h, number).start()
        return carry

    lax.fori_loop(0, heads, start_loads, 0)

    for copy in whole_loads:
        copy.wait()
    positions = lax.broadcasted_iota(jnp.int32, (1, rows), 1)
    lowest = jnp.maximum(
        start_own[...].reshape(1, rows) - here * rows,
        positions - window_own[...].reshape(1, rows) + 1,
    )
    stats_own[0:heads, :] = lse_own[...] * LOG2E
    model = heads * HEAD
    picks = (
        lax.broadcasted_iota(jnp.int32, (heads, model), 1) // HEAD
        == lax.broadcasted_iota(jnp.int32, (heads, model), 0)
    ).astype(jnp.float32).astype(jnp.bfloat16)
    for r in range(0, rows, 128):
        products = o_all[r : r + 128, :].astype(jnp.float32) * g_all[r : r + 128, :].astype(
            jnp.float32
        )
        high = products.astype(jnp.bfloat16)
        low = (products - high.astype(jnp.float32)).astype(jnp.bfloat16)
        stats_own[heads : 2 * heads, r : r + 128] = dot(picks, high, (1, 1)) + dot(
            picks, low, (1, 1)
        )
    stats_own[2 * heads : 2 * heads + 8, :] = jnp.broadcast_to(
        (lowest + rows).astype(jnp.float32), (8, rows)
    )

    @pl.when(has_before)
    def _():
        stats_copy.start()

    def settle(h, carry):
        for number in range(4):
            head_load(h, number).wait()

        return carry

    lax.fori_loop(0, heads, settle, 0)
    for h in range(TURNED + EARLY, TURNED + AHEAD):
        admit(h)

    key_at = lax.broadcasted_iota(jnp.int32, (half, half), 0)
    query_at = lax.broadcasted_iota(jnp.int32, (half, half), 1)

    def hidden_where_not(mask):
        return jnp.where(mask, 0.0, HIDDEN)

    bias[0] = hidden_where_not((key_at >= lowest[:, lo]) & (key_at <= query_at))
    bias[1] = hidden_where_not(key_at >= lowest[:, hi])
    bias[2] = hidden_where_not((key_at + half >= lowest[:, hi]) & (key_at <= query_at))

    bias[6] = hidden_where_not(key_at - half >= lowest[:, lo])
    bias[7] = hidden_where_not(key_at - rows >= lowest[:, lo])
    bias[8] = hidden_where_not(key_at - half >= lowest[:, hi])

    def pair_block(k, v, q, g, lse, delta, number):
        s = dot(k, q, (1, 1)) * (scale * LOG2E) + bias[number]
        p = jnp.exp2(s - lse)
        ds = p * (dot(v, g, (1, 1)) - delta)
        return p.astype(jnp.bfloat16), ds.astype(jnp.bfloat16)

    def local(h):
        k, v, q, g = k_own[h], v_own[h], q_own[h], g_own[h]
        kt = k.T
        lse = stats_own[pl.ds(h, 1), :]
        delta = stats_own[pl.ds(heads + h, 1), :]

        def block(us, ts, number):
            return pair_block(k[us], v[us], q[ts], g[ts], lse[:, ts], delta[:, ts], number)

        p00, s00 = block(lo, lo, 0)
        p01, s01 = block(lo, hi, 1)
        p11, s11 = block(hi, hi, 2)
        slot = h
        dv_part[slot, lo] = dot(jnp.concatenate([p00, p01], axis=1), g, (1, 0))
        dv_part[slot, hi] = dot(p11, g[hi], (1, 0))
        dk_part[slot, lo] = dot(jnp.concatenate([s00, s01], axis=1), q, (1, 0))
        dk_part[slot, hi] = dot(s11, q[hi], (1, 0))
        dq_own[h, :, lo] = dot(kt[:, lo], s00, (1, 0))
        dq_own[h, :, hi] = dot(kt, jnp.concatenate([s01, s11], axis=0), (1, 0))

    def shared(h):
        k, v, q, g = k_own[h], v_own[h], q_next[h], g_next[h]
        kt = k.T
        lse = stats_next[pl.ds(h, 1), :]
        delta = stats_next[pl.ds(heads + h, 1), :]

        def block(us, ts, number):
            return pair_block(k[us], v[us], q[ts], g[ts], lse[:, ts], delta[:, ts], number)

        p10, s10 = block(hi, lo, 3)
        p00, s00 = block(lo, lo, 4)
        p11, s11 = block(hi, hi, 5)
        dq_sent[h, :, lo] = dot(kt, jnp.concatenate([s00, s10], axis=0), (1, 0)).astype(
            jnp.bfloat16
        )
        dq_sent[h, :, hi] = dot(kt[:, hi], s11, (1, 0)).astype(jnp.bfloat16)
        slot = h
        cols = columns(h)
        dv0 = dv_part[slot, lo] + dot(p00, g[lo], (1, 0))
        dv1 = dv_part[slot, hi] + dot(jnp.concatenate([p10, p11], axis=1), g, (1, 0))
        dk0 = dk_part[slot, lo] + dot(s00, q[lo], (1, 0))
        dk1 = dk_part[slot, hi] + dot(jnp.concatenate([s10, s11], axis=1), q, (1, 0))
        dv_out[lo, cols] = dv0.astype(jnp.bfloat16)
        dv_out[hi, cols] = dv1.astype(jnp.bfloat16)
        dk_out[lo, cols] = (dk0 * scale).astype(jnp.bfloat16)
        dk_out[hi, cols] = (dk1 * scale).astype(jnp.bfloat16)

    def turned(h):
        for copy in keys_to_after(h):
            copy.wait_recv()
        k, v, q, g = k_before[h], v_before[h], q_own[h], g_own[h]
        kt = k.T
        lse = stats_own[pl.ds(h, 1), :]
        delta = stats_own[pl.ds(heads + h, 1), :]

        def block(us, ts, number):
            return pair_block(k[us], v[us], q[ts], g[ts], lse[:, ts], delta[:, ts], number)

        p10, s10 = block(hi, lo, 6)
        p00, s00 = block(lo, lo, 7)
        p11, s11 = block(hi, hi, 8)
        dq_own[h, :, lo] += dot(kt, jnp.concatenate([s00, s10], axis=0), (1, 0))
        dq_own[h, :, hi] += dot(kt[:, hi], s11, (1, 0))
        dv0 = dot(p00, g[lo], (1, 0))
        dv1 = dot(jnp.concatenate([p10, p11], axis=1), g, (1, 0))
        dk0 = dot(s00, q[lo], (1, 0))
        dk1 = dot(jnp.concatenate([s10, s11], axis=1), q, (1, 0))
        dv_sent[h, lo] = dv0.astype(jnp.bfloat16)
        dv_sent[h, hi] = dv1.astype(jnp.bfloat16)
        dk_sent[h, lo] = dk0.astype(jnp.bfloat16)
        dk_sent[h, hi] = dk1.astype(jnp.bfloat16)

    def finish_turned(h):
        @pl.when(has_after)
        def _():
            for copy in grads_to_before(h):
                copy.wait_recv()
            dk_part[h] += dk_got[h].astype(jnp.float32)
            dv_part[h] += dv_got[h].astype(jnp.float32)

        dk_out[:, columns(h)] = (dk_part[h] * scale).astype(jnp.bfloat16)
        dv_out[:, columns(h)] = dv_part[h].astype(jnp.bfloat16)

    def finish(h):
        @pl.when(has_before)
        def _():
            to_after(h).wait_recv()

        total = (dq_own[h] + dq_got[h].astype(jnp.float32)) * scale
        dq_out[:, columns(h)] = total.T.astype(jnp.bfloat16)

    def leave(number):
        if number == 0:
            pl.semaphore_wait(ready_sem, 1)
        for copy in to_relay(leaves - detoured + number):
            copy.start()

    @pl.when(detours & (z > 0))
    def _():
        for number in range(PLAIN):
            leave(number)

    def lead(h, carry):
        local(h)
        return carry

    lax.fori_loop(0, TURNED + LEAD, lead, 0)

    @pl.when(detours & (z == 0))
    def _():
        leave(0)

    @pl.when(has_after)
    def _():
        stats_copy.wait_recv()

    @pl.when(jnp.logical_not(has_after))
    def _():
        stats_next[...] = jnp.full_like(stats_next, 2.0 * rows)

        def clear(h, carry):
            q_next[h] = jnp.zeros((rows, HEAD), jnp.bfloat16)
            g_next[h] = jnp.zeros((rows, HEAD), jnp.bfloat16)
            return carry

        lax.fori_loop(0, heads, clear, 0)

    @pl.when(jnp.logical_not(has_before))
    def _():
        def clear(h, carry):
            dq_got[h] = jnp.zeros((HEAD, rows), jnp.bfloat16)
            return carry

        lax.fori_loop(0, heads, clear, 0)

    bound = stats_next[2 * heads : 2 * heads + 1, :].astype(jnp.int32)
    bias[3] = hidden_where_not(key_at + half >= bound[:, lo])
    bias[4] = hidden_where_not(key_at >= bound[:, lo])
    bias[5] = hidden_where_not(key_at + half >= bound[:, hi])

    def step(h, more):
        item = h - TURNED

        @pl.when(has_before & (item < direct))
        def _():
            for copy in to_before(direct_head(item)):
                copy.wait_send()

        @pl.when(item + AHEAD < direct)
        def _():
            admit(direct_head(item + AHEAD))

        @pl.when(has_before & (item + AHEAD >= direct) & (item + AHEAD < direct + TURNED))
        def _():
            for copy in grads_to_before(item + AHEAD - direct):
                copy.start()

        for number in range(1, WRAPPED):

            @pl.when(detours & (z == 0) & (item == PACE * number - 1))
            def _():
                leave(number)

        for slot in range(WRAPPED + PLAIN):
            wanted, copies = forwards(slot)

            @pl.when(wanted & (item == FORWARDED[slot]))
            def _():
                for copy in arrived(slot):
                    copy.wait_recv()
                for copy in copies:
                    copy.start()

        @pl.when(has_after)
        def _():
            for copy in to_before(h):
                copy.wait_recv()

        shared(h)
        if more:
            local(h + LEAD)

        @pl.when(has_after)
        def _():
            to_after(h).start()

        @pl.when((h > TURNED) & (h <= 2 * TURNED))
        def _():
            @pl.when(has_before)
            def _():
                turned(h - TURNED - 1)

            dq_out[:, columns(h - TURNED - 1)] = (
                (dq_own[h - TURNED - 1] * scale).T.astype(jnp.bfloat16)
            )

        @pl.when(h >= TURNED + LAG)
        def _():
            finish(h - LAG)

    def both(h, carry):
        step(h, True)
        return carry

    def shared_only(h, carry):
        step(h, False)
        return carry

    lax.fori_loop(TURNED, heads - LEAD, both, 0)
    lax.fori_loop(heads - LEAD, heads, shared_only, 0)

    def drain(h, carry):
        @pl.when(has_after & (h >= TURNED))
        def _():
            to_after(h).wait_send()

        @pl.when(has_after & (h < TURNED))
        def _():
            for copy in keys_to_after(h):
                copy.wait_send()

        return carry

    lax.fori_loop(0, heads, drain, 0)

    @pl.when(detours)
    def _():
        def left(h, carry):
            for copy in to_relay(h):
                copy.wait_send()
            return carry

        lax.fori_loop(leaves - detoured, leaves, left, 0)

    for slot in range(WRAPPED + PLAIN):
        wanted, copies = forwards(slot)

        @pl.when(wanted)
        def _():
            for copy in copies:
                copy.wait_send()

    @pl.when(has_before)
    def _():
        stats_copy.wait_send()

    def finish_all_turned():
        lax.fori_loop(0, TURNED, lambda h, c: (finish_turned(h), c)[1], 0)

    @pl.when(core == 0)
    def _():
        finish_all_turned()

    lax.fori_loop(heads - LAG, heads, lambda h, c: (finish(h), c)[1], 0)

    @pl.when(core == 1)
    def _():
        finish_all_turned()


    @pl.when(has_before)
    def _():
        for h in range(TURNED):
            for copy in grads_to_before(h):
                copy.wait_send()


def write_out(*refs):
    sources, targets, sem = refs[:3], refs[3:6], refs[6]
    copies = [
        pltpu.make_async_copy(source, target, sem.at[number])
        for number, (source, target) in enumerate(zip(sources, targets))
    ]
    for copy in copies:
        copy.start()
    for copy in copies:
        copy.wait()


def solution(mesh):
    groups, group_size = mesh.shape["grp"], mesh.shape["seq"]

    def local(q, k, v, o, g, lse, start, window):
        rows, model = q.shape
        heads = lse.shape[0]
        block = pltpu.VMEM((rows, model), jnp.bfloat16)
        per_head = pltpu.VMEM((heads, rows, HEAD), jnp.bfloat16)
        turned = pltpu.VMEM((heads, HEAD, rows), jnp.bfloat16)
        stats = pltpu.VMEM((2 * heads + 8, rows), jnp.float32)
        part = pltpu.VMEM((heads, rows, HEAD), jnp.float32)
        few = pltpu.VMEM((TURNED, rows, HEAD), jnp.bfloat16)
        relay = pltpu.VMEM((WRAPPED + PLAIN, rows, HEAD), jnp.bfloat16)
        results = pl.pallas_call(
            functools.partial(kernel, groups, group_size, heads),
            out_shape=(block, block, block),
            in_specs=[pl.BlockSpec(memory_space=pl.ANY)] * 8,
            out_specs=(pl.BlockSpec(memory_space=pltpu.VMEM),) * 3,
            scratch_shapes=[
                per_head,
                per_head,
                per_head,
                per_head,
                block,
                block,
                pltpu.VMEM((heads, rows), jnp.float32),
                pltpu.VMEM((rows,), jnp.int32),
                pltpu.VMEM((rows,), jnp.int32),
                stats,
                stats,
                pltpu.VMEM((9, rows // 2, rows // 2), jnp.float32),
                per_head,
                per_head,
                part,
                part,
                pltpu.VMEM((heads, HEAD, rows), jnp.float32),
                turned,
                turned,
                few,
                few,
                few,
                few,
                few,
                few,
                relay,
                relay,
                pltpu.SemaphoreType.DMA((5,)),
                pltpu.SemaphoreType.DMA((4, heads)),
                pltpu.SemaphoreType.DMA((2, heads)),
                pltpu.SemaphoreType.DMA((2, heads)),
                pltpu.SemaphoreType.DMA((2,)),
                pltpu.SemaphoreType.DMA((heads,)),
                pltpu.SemaphoreType.DMA((heads,)),
                pltpu.SemaphoreType.DMA((2, TURNED)),
                pltpu.SemaphoreType.DMA((2, TURNED)),
                pltpu.SemaphoreType.DMA((2, TURNED)),
                pltpu.SemaphoreType.DMA((2, TURNED)),
                pltpu.SemaphoreType.DMA((2, WRAPPED + PLAIN)),
                pltpu.SemaphoreType.DMA((2, WRAPPED + PLAIN)),
                pltpu.SemaphoreType.DMA((2, WRAPPED + PLAIN)),
                pltpu.SemaphoreType.REGULAR,
            ],
            compiler_params=pltpu.CompilerParams(
                collective_id=0, has_side_effects=True, vmem_limit_bytes=48 * 2**20
            ),
        )(q, k, v, o, g, lse, start, window)
        return pl.pallas_call(
            write_out,
            out_shape=(jax.ShapeDtypeStruct((rows, model), jnp.bfloat16),) * 3,
            in_specs=[pl.BlockSpec(memory_space=pltpu.VMEM)] * 3,
            out_specs=(pl.BlockSpec(memory_space=pl.ANY),) * 3,
            scratch_shapes=[pltpu.SemaphoreType.DMA((3,))],
            compiler_params=pltpu.CompilerParams(vmem_limit_bytes=8 * 2**20),
        )(*(pltpu.with_memory_space_constraint(r, pltpu.VMEM) for r in results))

    block = P(("grp", "seq"), None)
    return jax.shard_map(
        local,
        mesh=mesh,
        in_specs=(block,) * 5 + (P(None, ("grp", "seq")),) + (P(("grp", "seq")),) * 2,
        out_specs=(block,) * 3,
        check_vma=False,
    )
```

```python
import functools

import jax
import jax.numpy as jnp
from jax import lax
from jax.experimental import pallas as pl
from jax.experimental.pallas import tpu as pltpu
from jax.sharding import PartitionSpec as P

MESH = pl.DeviceIdType.MESH
LOG2E = 1.4426950408889634
HEAD = 128
LEAD = 2
AHEAD = 4
LAG = 9
TURNED = 3
WRAPPED = 3
PLAIN = 1
PACE = 2
FORWARDED = (4, 6, 8, 2)
LATE = 2
EARLY = 3
HIDDEN = -1e30


def dot(a, b, contract):
    return lax.dot_general(
        a, b, ((contract[:1], contract[1:]), ((), ())), preferred_element_type=jnp.float32
    )


def kernel(
    groups,
    group_size,
    heads,
    q_hbm,
    k_hbm,
    v_hbm,
    o_hbm,
    g_hbm,
    lse_hbm,
    start_hbm,
    window_hbm,
    dq_out,
    dk_out,
    dv_out,
    q_own,
    k_own,
    v_own,
    g_own,
    o_all,
    g_all,
    lse_own,
    start_own,
    window_own,
    stats_own,
    stats_next,
    bias,
    q_next,
    g_next,
    dk_part,
    dv_part,
    dq_own,
    dq_sent,
    dq_got,
    k_before,
    v_before,
    dk_sent,
    dv_sent,
    dk_got,
    dv_got,
    q_relay,
    g_relay,
    load_sem,
    head_sem,
    send_sem,
    recv_sem,
    stats_sem,
    back_send_sem,
    back_recv_sem,
    keys_send_sem,
    keys_recv_sem,
    grads_send_sem,
    grads_recv_sem,
    relay_send_sem,
    relay_recv_sem,
    forward_send_sem,
    ready_sem,
):
    rows = q_hbm.shape[0]
    half = rows // 2
    count = groups * group_size
    here = lax.axis_index("grp") * group_size + lax.axis_index("seq")
    has_before, has_after = here > 0, here < count - 1
    scale = HEAD**-0.5
    lo, hi = slice(0, half), slice(half, rows)

    def place(index):
        return (index // group_size, lax.rem(index, group_size))

    before = place(lax.rem(here + count - 1, count))
    after = place(lax.rem(here + 1, count))

    core = lax.rem(here, 2)
    z = lax.rem(here // 2, 4)
    ring = here - 2 * z - core
    even_z = lax.rem(z, 2) == 0
    detours = (core == 0) & has_before
    detoured = jnp.where(detours, jnp.where(z == 0, WRAPPED, PLAIN), 0)
    direct = heads - TURNED - detoured
    leaves = heads - LATE
    relay_of_here = place(ring + 2 * lax.rem(z + jnp.where(even_z, 2, 1), 4) + 1)
    relays = (core == 1) & even_z
    first_client = ring + 2 * lax.rem(z + 2, 4)
    second_client = ring + 2 * lax.rem(z + 3, 4)
    relays_first = relays & (first_client > 0)
    first_count = jnp.where(z == 2, WRAPPED, PLAIN)
    next_z = lax.rem(z + 1, 4)
    next_ring = here + 1 - 2 * next_z
    relay_of_after = place(next_ring + 2 * lax.rem(next_z + jnp.where(even_z, 1, 2), 4) + 1)

    def columns(h):
        return pl.ds(pl.multiple_of(h * HEAD, HEAD), HEAD)

    def head_load(h, number):
        source, target = ((q_hbm, q_own), (g_hbm, g_own), (k_hbm, k_own), (v_hbm, v_own))[number]
        return pltpu.make_async_copy(
            source.at[:, columns(h)], target.at[h], head_sem.at[number, h]
        )

    def to_before(h, early=False):
        return [
            pltpu.make_async_remote_copy(
                src_ref=origin.at[:, columns(h)] if early else source.at[h],
                dst_ref=target.at[h],
                send_sem=send_sem.at[number, h],
                recv_sem=recv_sem.at[number, h],
                device_id=before,
                device_id_type=MESH,
            )
            for number, (origin, source, target) in enumerate(
                ((q_hbm, q_own, q_next), (g_hbm, g_own, g_next))
            )
        ]

    def to_after(h):
        return pltpu.make_async_remote_copy(
            src_ref=dq_sent.at[h],
            dst_ref=dq_got.at[h],
            send_sem=back_send_sem.at[h],
            recv_sem=back_recv_sem.at[h],
            device_id=after,
            device_id_type=MESH,
        )

    def keys_to_after(h):
        return [
            pltpu.make_async_remote_copy(
                src_ref=source.at[:, columns(h)],
                dst_ref=target.at[h],
                send_sem=keys_send_sem.at[number, h],
                recv_sem=keys_recv_sem.at[number, h],
                device_id=after,
                device_id_type=MESH,
            )
            for number, (source, target) in enumerate(((k_hbm, k_before), (v_hbm, v_before)))
        ]

    def grads_to_before(h):
        return [
            pltpu.make_async_remote_copy(
                src_ref=source.at[h],
                dst_ref=target.at[h],
                send_sem=grads_send_sem.at[number, h],
                recv_sem=grads_recv_sem.at[number, h],
                device_id=before,
                device_id_type=MESH,
            )
            for number, (source, target) in enumerate(((dk_sent, dk_got), (dv_sent, dv_got)))
        ]

    def to_relay(h):
        slot = h - (leaves - detoured) + jnp.where(even_z, 0, WRAPPED)
        return [
            pltpu.make_async_remote_copy(
                src_ref=source.at[h],
                dst_ref=target.at[slot],
                send_sem=relay_send_sem.at[number, slot],
                recv_sem=relay_recv_sem.at[number, slot],
                device_id=relay_of_here,
                device_id_type=MESH,
            )
            for number, (source, target) in enumerate(((q_own, q_relay), (g_own, g_relay)))
        ]

    def forward(slot, h, client):
        return [
            pltpu.make_async_remote_copy(
                src_ref=source.at[slot],
                dst_ref=target.at[h],
                send_sem=forward_send_sem.at[number, slot],
                recv_sem=recv_sem.at[number, h],
                device_id=place(client - 1),
                device_id_type=MESH,
            )
            for number, (source, target) in enumerate(((q_relay, q_next), (g_relay, g_next)))
        ]

    def forwards(slot):
        if slot < WRAPPED:
            wanted = relays_first & (slot < first_count)
            return wanted, forward(slot, leaves - first_count + slot, first_client)
        return relays, forward(slot, leaves - PLAIN + slot - WRAPPED, second_client)

    def arrived(slot):
        return [
            pltpu.make_async_remote_copy(
                src_ref=source.at[0],
                dst_ref=target.at[slot],
                send_sem=relay_send_sem.at[number, slot],
                recv_sem=relay_recv_sem.at[number, slot],
                device_id=before,
                device_id_type=MESH,
            )
            for number, (source, target) in enumerate(((q_own, q_relay), (g_own, g_relay)))
        ]

    stats_copy = pltpu.make_async_remote_copy(
        src_ref=stats_own.at[8:],
        dst_ref=stats_next.at[8:],
        send_sem=stats_sem.at[0],
        recv_sem=stats_sem.at[1],
        device_id=before,
        device_id_type=MESH,
    )

    whole_loads = [
        pltpu.make_async_copy(source, target, load_sem.at[number])
        for number, (source, target) in enumerate(
            (
                (o_hbm, o_all),
                (g_hbm, g_all),
                (lse_hbm, lse_own),
                (start_hbm, start_own),
                (window_hbm, window_own),
            )
        )
    ]
    barrier = pltpu.get_barrier_semaphore()

    def greet(wanted, device):
        @pl.when(wanted)
        def _():
            pl.semaphore_signal(barrier, inc=1, device_id=device, device_id_type=MESH)

    greet(has_after, after)
    greet(has_before, before)
    greet(detours, relay_of_here)
    greet((core == 1) & has_after, relay_of_after)

    for copy in whole_loads:
        copy.start()

    pl.semaphore_wait(
        barrier,
        has_before.astype(jnp.int32)
        + has_after.astype(jnp.int32)
        + 2 * relays.astype(jnp.int32)
        + 2 * relays_first.astype(jnp.int32),
    )

    @pl.when(relays_first)
    def _():
        pl.semaphore_signal(
            ready_sem, inc=1, device_id=place(first_client), device_id_type=MESH
        )

    @pl.when(relays)
    def _():
        pl.semaphore_signal(
            ready_sem, inc=1, device_id=place(second_client), device_id_type=MESH
        )

    def direct_head(item):
        h = TURNED + item
        return jnp.where(h < leaves - detoured, h, h + detoured)

    def admit(h, early=False):
        @pl.when(has_before)
        def _():
            for copy in to_before(h, early):
                copy.start()

    for h in range(TURNED, TURNED + EARLY):
        admit(h, True)

    @pl.when(has_after)
    def _():
        for h in range(TURNED):
            for copy in keys_to_after(h):
                copy.start()

    def start_loads(h, carry):
        for number in range(4):
            head_load(h, number).start()
        return carry

    lax.fori_loop(0, heads, start_loads, 0)

    for copy in whole_loads:
        copy.wait()
    positions = lax.broadcasted_iota(jnp.int32, (1, rows), 1)
    lowest = jnp.maximum(
        start_own[...].reshape(1, rows) - here * rows,
        positions - window_own[...].reshape(1, rows) + 1,
    )
    stats_own[0:TURNED, :] = lse_own[0:TURNED, :] * LOG2E
    stats_own[8 : 5 + heads, :] = lse_own[TURNED:heads, :] * LOG2E
    model = heads * HEAD
    picks = (
        lax.broadcasted_iota(jnp.int32, (heads, model), 1) // HEAD
        == lax.broadcasted_iota(jnp.int32, (heads, model), 0)
    ).astype(jnp.float32).astype(jnp.bfloat16)
    for r in range(0, rows, 128):
        products = o_all[r : r + 128, :].astype(jnp.float32) * g_all[r : r + 128, :].astype(
            jnp.float32
        )
        high = products.astype(jnp.bfloat16)
        low = (products - high.astype(jnp.float32)).astype(jnp.bfloat16)
        sums = dot(picks, high, (1, 1)) + dot(picks, low, (1, 1))
        stats_own[TURNED : 2 * TURNED, r : r + 128] = sums[0:TURNED]
        stats_own[5 + heads : 2 + 2 * heads, r : r + 128] = sums[TURNED:heads]
    stats_own[2 + 2 * heads : 8 + 2 * heads, :] = jnp.broadcast_to(
        (lowest + rows).astype(jnp.float32), (6, rows)
    )

    @pl.when(has_before)
    def _():
        stats_copy.start()

    def settle(h, carry):
        for number in range(4):
            head_load(h, number).wait()

        return carry

    lax.fori_loop(0, heads, settle, 0)
    for h in range(TURNED + EARLY, TURNED + AHEAD):
        admit(h)

    key_at = lax.broadcasted_iota(jnp.int32, (half, half), 0)
    query_at = lax.broadcasted_iota(jnp.int32, (half, half), 1)

    def hidden_where_not(mask):
        return jnp.where(mask, 0.0, HIDDEN)

    bias[0] = hidden_where_not((key_at >= lowest[:, lo]) & (key_at <= query_at))
    bias[1] = hidden_where_not(key_at >= lowest[:, hi])
    bias[2] = hidden_where_not((key_at + half >= lowest[:, hi]) & (key_at <= query_at))

    bias[6] = hidden_where_not(key_at - half >= lowest[:, lo])
    bias[7] = hidden_where_not(key_at - rows >= lowest[:, lo])
    bias[8] = hidden_where_not(key_at - half >= lowest[:, hi])

    def lse_row(h):
        return jnp.where(h < TURNED, h, h + 5)

    def delta_row(h):
        return jnp.where(h < TURNED, h + TURNED, h + heads + 2)

    def pair_block(k, v, q, g, lse, delta, number):
        s = dot(k, q, (1, 1)) * (scale * LOG2E) + bias[number]
        p = jnp.exp2(s - lse)
        ds = p * (dot(v, g, (1, 1)) - delta)
        return p.astype(jnp.bfloat16), ds.astype(jnp.bfloat16)

    def local(h):
        k, v, q, g = k_own[h], v_own[h], q_own[h], g_own[h]
        kt = k.T
        lse = stats_own[pl.ds(lse_row(h), 1), :]
        delta = stats_own[pl.ds(delta_row(h), 1), :]

        def block(us, ts, number):
            return pair_block(k[us], v[us], q[ts], g[ts], lse[:, ts], delta[:, ts], number)

        p00, s00 = block(lo, lo, 0)
        p01, s01 = block(lo, hi, 1)
        p11, s11 = block(hi, hi, 2)
        slot = h
        dv_part[slot, lo] = dot(jnp.concatenate([p00, p01], axis=1), g, (1, 0))
        dv_part[slot, hi] = dot(p11, g[hi], (1, 0))
        dk_part[slot, lo] = dot(jnp.concatenate([s00, s01], axis=1), q, (1, 0))
        dk_part[slot, hi] = dot(s11, q[hi], (1, 0))
        dq_own[h, :, lo] = dot(kt[:, lo], s00, (1, 0))
        dq_own[h, :, hi] = dot(kt, jnp.concatenate([s01, s11], axis=0), (1, 0))

    def shared(h):
        k, v, q, g = k_own[h], v_own[h], q_next[h], g_next[h]
        kt = k.T
        lse = stats_next[pl.ds(lse_row(h), 1), :]
        delta = stats_next[pl.ds(delta_row(h), 1), :]

        def block(us, ts, number):
            return pair_block(k[us], v[us], q[ts], g[ts], lse[:, ts], delta[:, ts], number)

        p10, s10 = block(hi, lo, 3)
        p00, s00 = block(lo, lo, 4)
        p11, s11 = block(hi, hi, 5)
        dq_sent[h, :, lo] = dot(kt, jnp.concatenate([s00, s10], axis=0), (1, 0)).astype(
            jnp.bfloat16
        )
        dq_sent[h, :, hi] = dot(kt[:, hi], s11, (1, 0)).astype(jnp.bfloat16)
        slot = h
        cols = columns(h)
        dv0 = dv_part[slot, lo] + dot(p00, g[lo], (1, 0))
        dv1 = dv_part[slot, hi] + dot(jnp.concatenate([p10, p11], axis=1), g, (1, 0))
        dk0 = dk_part[slot, lo] + dot(s00, q[lo], (1, 0))
        dk1 = dk_part[slot, hi] + dot(jnp.concatenate([s10, s11], axis=1), q, (1, 0))
        dv_out[lo, cols] = dv0.astype(jnp.bfloat16)
        dv_out[hi, cols] = dv1.astype(jnp.bfloat16)
        dk_out[lo, cols] = (dk0 * scale).astype(jnp.bfloat16)
        dk_out[hi, cols] = (dk1 * scale).astype(jnp.bfloat16)

    def turned(h):
        for copy in keys_to_after(h):
            copy.wait_recv()
        k, v, q, g = k_before[h], v_before[h], q_own[h], g_own[h]
        kt = k.T
        lse = stats_own[pl.ds(lse_row(h), 1), :]
        delta = stats_own[pl.ds(delta_row(h), 1), :]

        def block(us, ts, number):
            return pair_block(k[us], v[us], q[ts], g[ts], lse[:, ts], delta[:, ts], number)

        p10, s10 = block(hi, lo, 6)
        p00, s00 = block(lo, lo, 7)
        p11, s11 = block(hi, hi, 8)
        dq_own[h, :, lo] += dot(kt, jnp.concatenate([s00, s10], axis=0), (1, 0))
        dq_own[h, :, hi] += dot(kt[:, hi], s11, (1, 0))
        dv0 = dot(p00, g[lo], (1, 0))
        dv1 = dot(jnp.concatenate([p10, p11], axis=1), g, (1, 0))
        dk0 = dot(s00, q[lo], (1, 0))
        dk1 = dot(jnp.concatenate([s10, s11], axis=1), q, (1, 0))
        dv_sent[h, lo] = dv0.astype(jnp.bfloat16)
        dv_sent[h, hi] = dv1.astype(jnp.bfloat16)
        dk_sent[h, lo] = dk0.astype(jnp.bfloat16)
        dk_sent[h, hi] = dk1.astype(jnp.bfloat16)

    def finish_turned(h):
        @pl.when(has_after)
        def _():
            for copy in grads_to_before(h):
                copy.wait_recv()
            dk_part[h] += dk_got[h].astype(jnp.float32)
            dv_part[h] += dv_got[h].astype(jnp.float32)

        dk_out[:, columns(h)] = (dk_part[h] * scale).astype(jnp.bfloat16)
        dv_out[:, columns(h)] = dv_part[h].astype(jnp.bfloat16)

    def finish(h):
        @pl.when(has_before)
        def _():
            to_after(h).wait_recv()

        total = (dq_own[h] + dq_got[h].astype(jnp.float32)) * scale
        dq_out[:, columns(h)] = total.T.astype(jnp.bfloat16)

    def leave(number):
        if number == 0:
            pl.semaphore_wait(ready_sem, 1)
        for copy in to_relay(leaves - detoured + number):
            copy.start()

    @pl.when(detours & (z > 0))
    def _():
        for number in range(PLAIN):
            leave(number)

    def lead(h, carry):
        local(h)
        return carry

    lax.fori_loop(0, TURNED + LEAD, lead, 0)

    @pl.when(detours & (z == 0))
    def _():
        leave(0)

    @pl.when(has_after)
    def _():
        stats_copy.wait_recv()

    @pl.when(jnp.logical_not(has_after))
    def _():
        stats_next[...] = jnp.full_like(stats_next, 2.0 * rows)

        def clear(h, carry):
            q_next[h] = jnp.zeros((rows, HEAD), jnp.bfloat16)
            g_next[h] = jnp.zeros((rows, HEAD), jnp.bfloat16)
            return carry

        lax.fori_loop(0, heads, clear, 0)

    @pl.when(jnp.logical_not(has_before))
    def _():
        def clear(h, carry):
            dq_got[h] = jnp.zeros((HEAD, rows), jnp.bfloat16)
            return carry

        lax.fori_loop(0, heads, clear, 0)

    bound = stats_next[2 + 2 * heads : 3 + 2 * heads, :].astype(jnp.int32)
    bias[3] = hidden_where_not(key_at + half >= bound[:, lo])
    bias[4] = hidden_where_not(key_at >= bound[:, lo])
    bias[5] = hidden_where_not(key_at + half >= bound[:, hi])

    def step(h, more):
        item = h - TURNED

        @pl.when(has_before & (item < direct))
        def _():
            for copy in to_before(direct_head(item)):
                copy.wait_send()

        @pl.when(item + AHEAD < direct)
        def _():
            admit(direct_head(item + AHEAD))

        @pl.when(has_before & (item + AHEAD >= direct) & (item + AHEAD < direct + TURNED))
        def _():
            for copy in grads_to_before(item + AHEAD - direct):
                copy.start()

        for number in range(1, WRAPPED):

            @pl.when(detours & (z == 0) & (item == PACE * number - 1))
            def _():
                leave(number)

        for slot in range(WRAPPED + PLAIN):
            wanted, copies = forwards(slot)

            @pl.when(wanted & (item == FORWARDED[slot]))
            def _():
                for copy in arrived(slot):
                    copy.wait_recv()
                for copy in copies:
                    copy.start()

        @pl.when(has_after)
        def _():
            for copy in to_before(h):
                copy.wait_recv()

        shared(h)
        if more:
            local(h + LEAD)

        @pl.when(has_after)
        def _():
            to_after(h).start()

        @pl.when((h > TURNED) & (h <= 2 * TURNED))
        def _():
            @pl.when(has_before)
            def _():
                turned(h - TURNED - 1)

            dq_out[:, columns(h - TURNED - 1)] = (
                (dq_own[h - TURNED - 1] * scale).T.astype(jnp.bfloat16)
            )

        @pl.when(h >= TURNED + LAG)
        def _():
            finish(h - LAG)

    def both(h, carry):
        step(h, True)
        return carry

    def shared_only(h, carry):
        step(h, False)
        return carry

    lax.fori_loop(TURNED, heads - LEAD, both, 0)
    lax.fori_loop(heads - LEAD, heads, shared_only, 0)

    def drain(h, carry):
        @pl.when(has_after & (h >= TURNED))
        def _():
            to_after(h).wait_send()

        @pl.when(has_after & (h < TURNED))
        def _():
            for copy in keys_to_after(h):
                copy.wait_send()

        return carry

    lax.fori_loop(0, heads, drain, 0)

    @pl.when(detours)
    def _():
        def left(h, carry):
            for copy in to_relay(h):
                copy.wait_send()
            return carry

        lax.fori_loop(leaves - detoured, leaves, left, 0)

    for slot in range(WRAPPED + PLAIN):
        wanted, copies = forwards(slot)

        @pl.when(wanted)
        def _():
            for copy in copies:
                copy.wait_send()

    @pl.when(has_before)
    def _():
        stats_copy.wait_send()

    def finish_all_turned():
        lax.fori_loop(0, TURNED, lambda h, c: (finish_turned(h), c)[1], 0)

    @pl.when(core == 0)
    def _():
        finish_all_turned()

    lax.fori_loop(heads - LAG, heads, lambda h, c: (finish(h), c)[1], 0)

    @pl.when(core == 1)
    def _():
        finish_all_turned()


    @pl.when(has_before)
    def _():
        for h in range(TURNED):
            for copy in grads_to_before(h):
                copy.wait_send()


def write_out(*refs):
    sources, targets, sem = refs[:3], refs[3:6], refs[6]
    copies = [
        pltpu.make_async_copy(source, target, sem.at[number])
        for number, (source, target) in enumerate(zip(sources, targets))
    ]
    for copy in copies:
        copy.start()
    for copy in copies:
        copy.wait()


def solution(mesh):
    groups, group_size = mesh.shape["grp"], mesh.shape["seq"]

    def local(q, k, v, o, g, lse, start, window):
        rows, model = q.shape
        heads = lse.shape[0]
        block = pltpu.VMEM((rows, model), jnp.bfloat16)
        per_head = pltpu.VMEM((heads, rows, HEAD), jnp.bfloat16)
        turned = pltpu.VMEM((heads, HEAD, rows), jnp.bfloat16)
        stats = pltpu.VMEM((2 * heads + 8, rows), jnp.float32)
        part = pltpu.VMEM((heads, rows, HEAD), jnp.float32)
        few = pltpu.VMEM((TURNED, rows, HEAD), jnp.bfloat16)
        relay = pltpu.VMEM((WRAPPED + PLAIN, rows, HEAD), jnp.bfloat16)
        results = pl.pallas_call(
            functools.partial(kernel, groups, group_size, heads),
            out_shape=(block, block, block),
            in_specs=[pl.BlockSpec(memory_space=pl.ANY)] * 8,
            out_specs=(pl.BlockSpec(memory_space=pltpu.VMEM),) * 3,
            scratch_shapes=[
                per_head,
                per_head,
                per_head,
                per_head,
                block,
                block,
                pltpu.VMEM((heads, rows), jnp.float32),
                pltpu.VMEM((rows,), jnp.int32),
                pltpu.VMEM((rows,), jnp.int32),
                stats,
                stats,
                pltpu.VMEM((9, rows // 2, rows // 2), jnp.float32),
                per_head,
                per_head,
                part,
                part,
                pltpu.VMEM((heads, HEAD, rows), jnp.float32),
                turned,
                turned,
                few,
                few,
                few,
                few,
                few,
                few,
                relay,
                relay,
                pltpu.SemaphoreType.DMA((5,)),
                pltpu.SemaphoreType.DMA((4, heads)),
                pltpu.SemaphoreType.DMA((2, heads)),
                pltpu.SemaphoreType.DMA((2, heads)),
                pltpu.SemaphoreType.DMA((2,)),
                pltpu.SemaphoreType.DMA((heads,)),
                pltpu.SemaphoreType.DMA((heads,)),
                pltpu.SemaphoreType.DMA((2, TURNED)),
                pltpu.SemaphoreType.DMA((2, TURNED)),
                pltpu.SemaphoreType.DMA((2, TURNED)),
                pltpu.SemaphoreType.DMA((2, TURNED)),
                pltpu.SemaphoreType.DMA((2, WRAPPED + PLAIN)),
                pltpu.SemaphoreType.DMA((2, WRAPPED + PLAIN)),
                pltpu.SemaphoreType.DMA((2, WRAPPED + PLAIN)),
                pltpu.SemaphoreType.REGULAR,
            ],
            compiler_params=pltpu.CompilerParams(
                collective_id=0, has_side_effects=True, vmem_limit_bytes=48 * 2**20
            ),
        )(q, k, v, o, g, lse, start, window)
        return pl.pallas_call(
            write_out,
            out_shape=(jax.ShapeDtypeStruct((rows, model), jnp.bfloat16),) * 3,
            in_specs=[pl.BlockSpec(memory_space=pltpu.VMEM)] * 3,
            out_specs=(pl.BlockSpec(memory_space=pl.ANY),) * 3,
            scratch_shapes=[pltpu.SemaphoreType.DMA((3,))],
            compiler_params=pltpu.CompilerParams(vmem_limit_bytes=8 * 2**20),
        )(*(pltpu.with_memory_space_constraint(r, pltpu.VMEM) for r in results))

    block = P(("grp", "seq"), None)
    return jax.shard_map(
        local,
        mesh=mesh,
        in_specs=(block,) * 5 + (P(None, ("grp", "seq")),) + (P(("grp", "seq")),) * 2,
        out_specs=(block,) * 3,
        check_vma=False,
    )
```
